256 devices in a mesh: expert: 16 (over z, core), tensor: 16 (over y, x).
Axes of the slice: x: 4, y: 4, z: 8, core: 2. Of those that a mesh axis runs over, the one named last changes fastest.
Arguments:
- queries: bfloat16 [96, 2, 6144], P('expert'), may hold values from -20 to 20
- new_kv: bfloat16 [2, 96, 2, 1024], P(None, 'expert'), may hold values from -4 to 4
- cache: bfloat16 [2, 96, 8, 4096, 128], P(None, 'expert', None, 'tensor'), may hold values from -4 to 4
- residual: bfloat16 [96, 2, 6144], P('expert'), may hold values from -16 to 16
- w_out: bfloat16 [6144, 6144], P('tensor'), may hold values from -0.078125 to 0.078125
- norm_gain: float32 [6144], replicated, may hold values from 0.1 to 1.9
- routes: int32 [96, 2, 4], P('expert'), may hold values from 0 to 7, all different within a row; in each aligned block of 12 rows (0 to 11, 12 to 23, ..., all dimensions but the last counted through in order) at most 9 rows name the same one
- route_weight: float32 [96, 2, 4], P('expert'), may hold values from 0.1 to 0.6
- w_in: bfloat16 [16, 6144, 2, 2688], P('expert', None, None, 'tensor'), may hold values from -0.078125 to 0.078125
- w_down: bfloat16 [16, 2688, 6144], P('expert', 'tensor'), may hold values from -0.109375 to 0.109375
Outputs:
- mixed: bfloat16 [96, 2, 6144], P('expert', None, 'tensor')
The draws below stay inside these ranges and needn't reach their ends.
Inputs may be any that keep to these rules, and one draw needn't show every extreme that they name: `routes`: in each aligned block of 12 tokens (the rows of one index of expert) each expert is named at most 9 times; the 4 experts of a token differ.
All inputs are finite; a program needn't handle non-finite values.
Results may differ from the reference program's by a relative error of at most 0.014.
Values may be sent and summed in bfloat16 or wider, within the bound.
A program may use at most 128 MiB of HBM per device.

```python
import math
import jax
import jax.numpy as jnp
import numpy as np
from jax import lax

D = 6144
HEADS = 48
KV = 8
HD = 128
EXPERTS = 8
FF = 5376
TOP = 4
LEN = 4096
STEPS = 2
ROWS_DEV = 6
ROWS = 96
SLABS = 16
COPIES = 2
CAP = 9


def attention_data(key, scale_low, scale_high):
    pieces = jax.random.split(key, 8)
    new_kv = jnp.clip(jax.random.normal(pieces[0], (2, ROWS, STEPS, KV * HD)), -4.0, 4.0)
    base = jnp.clip(jax.random.normal(pieces[1], (2, ROWS, KV, LEN, HD)), -4.0, 4.0)
    scales = jnp.exp(jax.random.uniform(pieces[2], (ROWS, KV, LEN, 1), minval=jnp.log(scale_low), maxval=jnp.log(scale_high)))
    cache_keys = jnp.clip(base[0] * scales, -4.0, 4.0)
    cache_values = jnp.clip(base[1], -4.0, 4.0)
    first = jax.random.randint(pieces[4], (ROWS, KV, 1, 1), 0, LEN)
    offset = jax.random.randint(pieces[5], (ROWS, KV, 1, 1), 1, LEN)
    second = (first + offset) % LEN
    anchor = jax.random.uniform(pieces[6], (ROWS, KV, 1, HD), minval=-4.0, maxval=4.0)
    levels = jnp.array([2.0, 3.0, 4.5], jnp.float32)
    strength = levels[jax.random.randint(pieces[7], (ROWS,), 0, 3)].reshape(ROWS, 1, 1, 1)
    shrink = 2.0 / (strength * (16.0 / 3.0) * HD ** 0.5)
    position = jnp.arange(LEN).reshape(1, 1, LEN, 1)
    cache_keys = jnp.where(position == first, anchor, cache_keys)
    cache_keys = jnp.where(position == second, anchor * (1.0 - shrink), cache_keys)
    cache = jnp.stack([cache_keys, cache_values])
    return (new_kv, cache, anchor[:, :, 0, :])


def draw_new_kv(key, part):
    return attention_data(key, 1.0, 1.0)[0].astype(jnp.bfloat16)


def draw_cache(key, part):
    return attention_data(key, 1.0, 1.0)[1].astype(jnp.bfloat16)


def draw_queries(key, part):
    new_kv, cache, anchor = attention_data(key, 1.0, 1.0)
    key = jax.random.fold_in(key, 7)
    pieces = jax.random.split(key, 2)
    noise = jnp.clip(jax.random.normal(pieces[0], (ROWS, STEPS, HEADS * HD)), -5.0, 5.0)
    groups = HEADS // KV
    own_keys = jnp.broadcast_to(new_kv[0].reshape(ROWS, STEPS, KV, 1, HD), (ROWS, STEPS, KV, groups, HD))
    queries = 2.0 * noise + 0.8 * own_keys.reshape(ROWS, STEPS, HEADS * HD)
    pull = 24.0 / (16.0 / 3.0 * HD ** 0.5)
    toward = jnp.broadcast_to((pull * anchor).reshape(ROWS, 1, KV, 1, HD), (ROWS, STEPS, KV, groups, HD))
    picked = jax.random.randint(pieces[1], (ROWS, 1, KV, groups, 1), 0, 2).astype(jnp.float32)
    queries = (queries.reshape(ROWS, STEPS, KV, groups, HD) + picked * toward).reshape(ROWS, STEPS, HEADS * HD)
    return queries.astype(jnp.bfloat16)


def draw_residual(key, part):
    key = jax.random.fold_in(key, 5)
    pieces = jax.random.split(key, 1)
    ramp = 0.3 * (1.0 + 2.0 * jnp.arange(D, dtype=jnp.float32) / (D - 1))
    return (jnp.clip(jax.random.normal(pieces[0], (ROWS, STEPS, D)), -4.0, 4.0) * ramp).astype(jnp.bfloat16)


def raised(result, own_key, source, target, parts, factor):
    def block_of(dim):
        return (jnp.arange(result.shape[dim]) // (result.shape[dim] // parts)).reshape((-1,) + (1,) * (result.ndim - 1 - dim))

    one_side = jax.random.permutation(own_key, parts)[block_of(target)]
    far = (block_of(target) + parts // 2) % parts
    return jnp.where((block_of(source) == one_side) | (block_of(source) == far), factor * result, result)


def shard_levels(stream_key, shape, shards, least, top_value):
    def one(dim, blocks):
        steps = jax.random.uniform(jax.random.fold_in(jax.random.fold_in(stream_key, 6), dim), (blocks,), jnp.float32, least / len(shards), top_value / len(shards))
        return jnp.repeat(jnp.exp(steps), shape[dim] // blocks).reshape((-1,) + (1,) * (len(shape) - dim - 1))

    gain = one(*shards[0])
    for cut in shards[1:]:
        gain = gain * one(*cut)
    return gain


def routed_block(rng, own, number, rows, amount, top, most, slope):
    sequence = jax.random.permutation(rng, amount)
    crowded, ordinary = portions_of(amount, rows * top, most, slope, True), portions_of(amount, rows * top, most, slope, False)
    places = jnp.arange(amount)

    def named(tallies, rotation):
        used = int((tallies > 0).sum())
        fixed = max(1, used // 4)
        moved = fixed + (places - fixed + rotation * (used - fixed)) % max(1, amount - fixed)
        return jnp.zeros((amount,), jnp.int32).at[sequence[jnp.where(places < fixed, places, moved)]].set(jnp.asarray(tallies, jnp.int32))

    tallies = jnp.where(number % 4 == 0, named(crowded, number // 4), named(ordinary, number - number // 4 - 1))
    mixed = jax.random.permutation(jax.random.fold_in(own, 3), amount)
    source_of, sink = mixed[0:amount // 2 * 2:2], mixed[1:amount // 2 * 2:2]
    slack = jnp.minimum(tallies[source_of] - 1, most - tallies[sink]) // 2
    slack = jnp.where((source_of == sequence[0]) | (sink == sequence[0]) | (tallies[sink] == 0), 0, jnp.maximum(slack, 0))
    moved = jax.random.randint(jax.random.fold_in(own, 4), (amount // 2,), 0, 1 << 20) % (slack + 1)
    tallies = tallies.at[source_of].add(-moved).at[sink].add(moved)
    labels = jnp.searchsorted(jnp.cumsum(tallies), jnp.arange(rows * top), side="right").astype(jnp.int32)
    listing = labels.reshape(top, rows).T
    listing = listing[jax.random.permutation(jax.random.fold_in(own, 1), rows)]
    rotation = jax.random.randint(jax.random.fold_in(own, 2), (rows, 1), 0, top)
    return jnp.take_along_axis(listing, (jnp.arange(top)[None, :] + rotation) % top, axis=1)


def portions_of(number_of, total, most, lean, full):
    loads = [(1 << 20) // math.isqrt(standing ** lean) + 1 for standing in range(1, number_of + 1)]
    largest = most if full else min(most, max(-(-total // number_of), total * loads[0] // sum(loads)))
    least = 1 if total - largest >= number_of - 1 else 0
    given, surplus = [largest] + [least] * (number_of - 1), total - largest - least * (number_of - 1)
    while surplus > 0:
        free = [i for i in range(1, number_of) if given[i] < largest] or [i for i in range(1, number_of) if given[i] < most]
        pool, budget = sum([loads[i] for i in free]), surplus
        for i in free:
            more = min(most - given[i], max(1, budget * loads[i] // pool), surplus)
            given[i] = given[i] + more
            surplus = surplus - more
    return np.array(given)


def scatter_about(key, dims, deviation, limit, cuts=(), kind=jnp.bfloat16):
    gain = shard_levels(key, dims, cuts, -0.22, 0.18) if cuts else 1.0
    entries = jax.random.normal(key, dims, jnp.float32) * deviation * gain
    return jnp.minimum(jnp.maximum(entries, -limit), limit).astype(kind)


def noise_with(key, dims, width, most, cuts, heavy, held_as=jnp.bfloat16):
    values = width * jax.random.normal(key, dims, jnp.float32)
    if cuts:
        values = values * shard_levels(key, dims, cuts, -0.22, 0.18)
    return jnp.clip(raised(values, jax.random.fold_in(key, 3), *heavy), -most, most).astype(held_as)


def setup_inputs(seed: int = 0) -> dict:
    key_list = jax.random.split(jax.random.key(seed), 11)
    queries = draw_queries(jax.random.fold_in(key_list[10], 71), 0)
    new_kv = draw_new_kv(jax.random.fold_in(key_list[10], 71), 0)
    cache = draw_cache(jax.random.fold_in(key_list[10], 71), 0)
    residual = draw_residual(jax.random.fold_in(key_list[10], 71), 0)
    w_out = scatter_about(key_list[4], (HEADS * HD, D), (HEADS * HD) ** -0.5, 0.078125, ((0, 16),))
    norm_gain = jnp.clip(1.0 + 0.18 * jax.random.normal(key_list[5], (D,), jnp.float32), 0.1, 1.9)
    routes_keys = jax.random.split(jax.random.fold_in(key_list[6], 1), ROWS * STEPS // (ROWS_DEV * STEPS))
    routes_turns = jax.random.permutation(jax.random.fold_in(key_list[6], 3), ROWS * STEPS // (ROWS_DEV * STEPS))
    routes = jax.vmap(lambda own, number: routed_block(jax.random.fold_in(key_list[6], 2), own, number, ROWS_DEV * STEPS, EXPERTS, TOP, CAP, 2))(routes_keys, routes_turns).reshape((ROWS, STEPS, TOP))
    route_weight = jnp.clip(0.1 + 0.5 * jax.random.uniform(key_list[7], (ROWS, STEPS, TOP), jnp.float32) ** shard_levels(key_list[7], (ROWS, STEPS, TOP), ((0, 16),), -0.2, 0.2), 0.1, 0.6)
    w_in = scatter_about(key_list[8], (SLABS, D, 2, FF // COPIES), D ** -0.5, 0.078125, ((0, 16), (3, 16)))
    w_down = noise_with(key_list[9], (SLABS, FF // COPIES, D), FF ** -0.5, 0.109375, ((0, 16), (1, 16)), (1, 2, 16, 2.0))
    return {"queries": queries, "new_kv": new_kv, "cache": cache, "residual": residual, "w_out": w_out, "norm_gain": norm_gain, "routes": routes, "route_weight": route_weight, "w_in": w_in, "w_down": w_down}


norm_epsilon = 1e-05

def attend_row(inputs):
    query_row, new_keys, new_values, cache_keys, cache_values = inputs
    query_heads = query_row.astype(jnp.float32).reshape(STEPS, KV, HEADS // KV, HD)
    fresh_keys = new_keys.astype(jnp.float32).reshape(STEPS, KV, HD).transpose(1, 0, 2)
    fresh_values = new_values.astype(jnp.float32).reshape(STEPS, KV, HD).transpose(1, 0, 2)
    all_keys = jnp.concatenate([cache_keys.astype(jnp.float32), fresh_keys], axis=1)
    all_values = jnp.concatenate([cache_values.astype(jnp.float32), fresh_values], axis=1)
    scores = jnp.einsum('skgh,klh->skgl', query_heads, all_keys) * HD ** (-0.5)
    position = jnp.arange(LEN + STEPS, dtype=jnp.int32)
    allowed = position[None, :] < (LEN + 1 + jnp.arange(STEPS, dtype=jnp.int32))[:, None]
    scores = jnp.where(allowed[:, None, None, :], scores, -jnp.inf)
    row_max = lax.optimization_barrier(jnp.max(scores, axis=-1))
    weights = jnp.exp(scores - row_max[..., None])
    row_total = lax.optimization_barrier(jnp.sum(weights, axis=-1))
    weights_low = weights.astype(jnp.bfloat16).astype(jnp.float32)
    weighted = jnp.einsum('skgl,klh->skgh', weights_low, all_values)
    return (weighted / row_total[..., None]).astype(jnp.bfloat16).reshape(STEPS, HEADS * HD)

def reference(queries, new_kv, cache, residual, w_out, norm_gain, routes, route_weight, w_in, w_down):
    attended = lax.map(attend_row, (queries, new_kv[0], new_kv[1], cache[0], cache[1]))
    tokens = ROWS * STEPS
    projected = jnp.dot(attended.reshape(tokens, HEADS * HD), w_out, preferred_element_type=jnp.float32)
    hidden_state = residual.reshape(tokens, D).astype(jnp.float32) + projected
    average = lax.optimization_barrier(jnp.mean(hidden_state, axis=1, keepdims=True))
    variance = lax.optimization_barrier(jnp.mean(jnp.square(hidden_state - average), axis=1, keepdims=True))
    normed = ((hidden_state - average) * lax.rsqrt(variance + norm_epsilon) * norm_gain).astype(jnp.bfloat16)
    flat_routes = routes.reshape(tokens, TOP)
    flat_weights = route_weight.reshape(tokens, TOP)

    def add_slab(running, inputs):
        pair_weight, down_weight, slab_index = inputs
        gate_values = jnp.dot(normed, pair_weight[:, 0, :], preferred_element_type=jnp.float32)
        up_values = jnp.dot(normed, pair_weight[:, 1, :], preferred_element_type=jnp.float32)
        expert_hidden = (jax.nn.silu(gate_values) * up_values).astype(jnp.bfloat16)
        slab_output = jnp.dot(expert_hidden, down_weight, preferred_element_type=jnp.float32)
        expert = slab_index // COPIES
        factor = lax.optimization_barrier(jnp.sum(jnp.where(flat_routes == expert, flat_weights, 0.0), axis=1))
        return (running + factor[:, None] * slab_output, None)
    expert_mix, ignored = lax.scan(add_slab, jnp.zeros((tokens, D), jnp.float32), (w_in, w_down, jnp.arange(SLABS, dtype=jnp.int32)))
    return (hidden_state + expert_mix).astype(jnp.bfloat16).reshape(ROWS, STEPS, D)
```

```python
import jax
import jax.numpy as jnp
from jax import lax
from jax.experimental import pallas as pl
from jax.experimental.pallas import tpu as pltpu
from jax.sharding import PartitionSpec as P

D = 6144
HEADS = 48
KV = 8
HD = 128
EXPERTS = 8
TOP = 4
CAP = 9
ROWS = 6
STEPS = 2
KEYS = 256
UNITS = 168
PART = 384
PACK = 80
EPS = 1e-05
BF = jnp.bfloat16
F32 = jnp.float32
MESH = pl.DeviceIdType.MESH
NT = (((1,), (1,)), ((), ()))
TN = (((0,), (0,)), ((), ()))


def wrap(value, size):
    return lax.rem(value + size, size)


def iota(shape, dim):
    return lax.broadcasted_iota(jnp.int32, shape, dim)


def dot(a, b, dims=None):
    if dims is None:
        return jnp.dot(a, b, preferred_element_type=F32)
    return lax.dot_general(a, b, dims, preferred_element_type=F32)


def kernel(
    q_ref, nkv_ref, cache_ref, res_ref, wout_hbm, gain_ref, routes_ref, rw_ref, win_hbm, wdn_hbm,
    out_ref,
    kv, wout, win, wdn,
    a_send, a_recv, stat, fcol, att, proj, b_send, b_recv,
    state, z_send, z_recv, xall, acc, vacc, hid,
    q_send, q_recv, g_send, g_recv, chip, m_send, m_recv, y_send, y_recv,
    kv_sem, w_sem,
    a_ss, a_rs, b_ss, b_rs, z_ss, z_rs, x1_ss, x1_rs, x2_ss, x2_rs, xp_ss, xp_rs,
    q_ss, q_rs, g_ss, g_rs, m_ss, m_rs, y_ss, y_rs,
):
    b = lax.axis_index("expert")
    t = lax.axis_index("tensor")
    z, c = lax.div(b, 2), lax.rem(b, 2)
    y, x = lax.div(t, 4), lax.rem(t, 4)
    partner = 2 * z + 1 - c
    m = (1 - c) * x + c * y
    g = (1 - c) * y + c * x

    def place(core, group, member):
        return (1 - core) * (4 * group + member) + core * (4 * member + group)

    def plane_peer(i, sign):
        return 4 * wrap(y + sign * lax.div(i, 4), 4) + wrap(x + sign * lax.rem(i, 4), 4)

    def remote(src, dst, ss, rs, dev):
        return pltpu.make_async_remote_copy(
            src_ref=src, dst_ref=dst, send_sem=ss, recv_sem=rs, device_id=dev, device_id_type=MESH
        )

    def loop(lo, hi, fn):
        def step(i, carry):
            fn(i)
            return carry
        lax.fori_loop(lo, hi, step, 0)

    def load_row(r):
        return [
            pltpu.make_async_copy(cache_ref.at[s, r], kv.at[s, r], kv_sem.at[s, r]) for s in range(2)
        ]

    def start_row(r):
        for copy in load_row(r):
            copy.start()

    loop(0, ROWS, start_row)
    w_copies = [
        pltpu.make_async_copy(wout_hbm, wout, w_sem.at[0]),
        pltpu.make_async_copy(win_hbm, win, w_sem.at[1]),
        pltpu.make_async_copy(wdn_hbm, wdn, w_sem.at[2]),
    ]
    for copy in w_copies:
        copy.start()

    barrier = pltpu.get_barrier_semaphore()

    def greet(dev):
        pl.semaphore_signal(barrier, inc=1, device_id=dev, device_id_type=MESH)

    loop(1, 16, lambda i: greet((b, plane_peer(i, 1))))
    loop(1, 8, lambda d: greet((2 * wrap(z + d, 8) + c, t)))
    greet((partner, t))

    first = t == 0
    row_id = iota((128, 16), 0)
    key_id = iota((128, 16), 1)
    fresh_ok = (
        (lax.div(row_id, 16) == lax.div(key_id, 2))
        & (lax.rem(key_id, 2) <= lax.rem(row_id, 2))
        & (jnp.broadcast_to(t, (128, 16)) == 0)
    )
    lane = iota((128, 128), 1)
    stat[...] = jnp.zeros_like(stat)

    def attend_pair(pair):
        halves = []
        for half in range(2):
            r = 2 * pair + half
            k_copy, v_copy = load_row(r)
            k_copy.wait()
            qr = q_ref[r]
            scores = jnp.concatenate(
                [dot(qr[16 * k : 16 * k + 16], kv[0, r, k], NT) for k in range(KV)], axis=0
            ) * (HD**-0.5)
            extra = dot(qr, nkv_ref[0, r], NT) * (HD**-0.5)
            extra = jnp.where(fresh_ok, extra, -jnp.inf)
            top = jnp.maximum(
                jnp.max(scores, axis=1, keepdims=True), jnp.max(extra, axis=1, keepdims=True)
            )
            top = jnp.ceil(top * 0.25) * 4.0
            weights = jnp.exp(scores - top)
            extra = jnp.exp(extra - top)
            total = jnp.sum(weights, axis=1, keepdims=True) + jnp.sum(extra, axis=1, keepdims=True)
            low = weights.astype(BF)
            v_copy.wait()
            mixed = jnp.concatenate(
                [dot(low[16 * k : 16 * k + 16], kv[1, r, k]) for k in range(KV)], axis=0
            ) + dot(extra.astype(BF), nkv_ref[1, r])
            stat[...] = jnp.where(lane == r, top, jnp.where(lane == 8 + r, total, stat[...]))
            halves.append(mixed.reshape(16, 8, 128))
        a_send[:, pl.ds(pl.multiple_of(16 * pair, 16), 16), :] = jnp.concatenate(
            halves, axis=1
        ).astype(BF)

    loop(0, 3, attend_pair)
    table = jnp.transpose(stat[...])[0:16, :].astype(BF)
    a_send[:, 48:64, :] = jnp.broadcast_to(table[None], (16, 16, 128))
    a_recv[t] = a_send[t]
    pl.semaphore_wait(barrier, 23)

    def a_copy(i):
        to = plane_peer(i, 1)
        return remote(a_send.at[to], a_recv.at[t], a_ss.at[i], a_rs.at[i], (b, to))

    loop(1, 16, lambda i: a_copy(i).start())

    slot_lane = iota((16, 128), 1)
    token_row = iota((16, 128), 0)
    lane_expert = lax.div(slot_lane, 16)
    chosen = jnp.zeros((16, 128), F32)
    factor = jnp.zeros((16, 128), F32)
    for k in range(TOP):
        hit = routes_ref[:, k : k + 1] == lane_expert
        chosen = jnp.where(hit, 1.0, chosen)
        factor = jnp.where(hit, rw_ref[:, k : k + 1], factor)
    below = (iota((16, 16), 1) < iota((16, 16), 0)).astype(BF)
    earlier = dot(below, chosen.astype(BF))
    here = (chosen > 0.5) & (earlier.astype(jnp.int32) == lax.rem(slot_lane, 16))
    dispatch = jnp.where(here, 1.0, 0.0).astype(BF)
    combine = jnp.where(here, factor, 0.0)
    combine_high = combine.astype(BF)
    combine_low = (combine - combine_high.astype(F32)).astype(BF)
    mine = pl.ds(pl.multiple_of(t * PART, 128), PART)
    res_sum = jnp.sum(res_ref[...].astype(F32), axis=1, keepdims=True)
    gain_mine = gain_ref[:, mine]
    pack_row, pack_lane = iota((PACK, 128), 0), iota((PACK, 128), 1)
    packing = jnp.where(
        (pack_row == CAP * lax.div(pack_lane, 16) + lax.rem(pack_lane, 16))
        & (lax.rem(pack_lane, 16) < CAP),
        1.0,
        0.0,
    ).astype(BF)
    acc[...] = jnp.zeros_like(acc)
    vacc[...] = jnp.zeros_like(vacc)
    att[...] = jnp.zeros_like(att)
    w_copies[0].wait()

    loop(1, 16, lambda i: a_copy(i).wait_recv())

    stats = a_recv[:, 48:64, :].astype(F32)
    tops, totals = stats[:, 0:8], stats[:, 8:16]
    top = jnp.max(tops, axis=0, keepdims=True)
    scale = jnp.exp(tops - top)
    whole = jnp.sum(scale * totals, axis=0, keepdims=True)
    scale = scale / jnp.maximum(whole, 1e-30)
    fcol[...] = jnp.transpose(scale.reshape(128, 128))
    columns = fcol[pl.ds(pl.multiple_of(8 * t, 8), 8), :]
    for pair in range(3):
        both = a_recv[:, 16 * pair : 16 * pair + 16, :].astype(F32)
        for half in range(2):
            r = 2 * pair + half
            joined = jnp.zeros((8, 128), F32)
            for s in range(16):
                joined += both[s, 8 * half : 8 * half + 8] * columns[:, 8 * s + r : 8 * s + r + 1]
            for h in range(3):
                att[2 * r : 2 * r + 2, 128 * h : 128 * h + 128] = joined[2 * h : 2 * h + 2]

    attended = att[...].astype(BF)
    proj_sum = jnp.zeros((16, 1), F32)
    for s in range(16):
        part = dot(attended, wout[:, PART * s : PART * s + PART])
        proj[s] = part
        proj_sum = proj_sum + jnp.sum(part, axis=1, keepdims=True)
    diagonal = jnp.sum(jnp.where(token_row == slot_lane, proj_sum, 0.0), axis=0, keepdims=True)
    high = diagonal.astype(BF).astype(F32)
    low = diagonal - high
    head = jnp.where(token_row == 12, high, jnp.where(token_row == 13, low, 0.0))

    def b_fill(s):
        part = proj[s]
        b_send[s] = (
            part + jnp.concatenate([head, jnp.zeros((16, PART - 128), F32)], axis=1)
        ).astype(BF)

    def b_copy(i):
        to = plane_peer(i, 1)
        return remote(b_send.at[to], b_recv.at[t], b_ss.at[i], b_rs.at[i], (b, to))

    def b_step(i):
        b_fill(plane_peer(i, 1))
        b_copy(i).start()

    loop(1, 16, b_step)
    b_fill(t)
    b_recv[t] = b_send[t]
    loop(1, 16, lambda i: b_copy(i).wait_recv())

    summed = jnp.sum(b_recv[...].astype(F32), axis=0)
    spread = jnp.where(token_row == slot_lane, summed[12:13, 0:128] + summed[13:14, 0:128], 0.0)
    mean = (jnp.sum(spread, axis=1, keepdims=True) + res_sum) * (1.0 / D)
    real = iota((16, PART), 0) < ROWS * STEPS
    hidden = jnp.where(real, summed + res_ref[:, mine].astype(F32), 0.0)
    state[...] = hidden
    scaled = jnp.where(real, (hidden - mean) * gain_mine, 0.0).astype(BF)

    z_send[...] = dot(dispatch, scaled, TN).astype(BF).reshape(EXPERTS, 16, PART)
    z_recv[z] = z_send[z]

    def z_copy(d):
        to = wrap(z + d, 8)
        return remote(z_send.at[to], z_recv.at[z], z_ss.at[d], z_rs.at[d], (2 * to + c, t))

    loop(1, 8, lambda d: z_copy(d).start())
    w_copies[1].wait()
    w_copies[2].wait()
    loop(1, 8, lambda d: z_copy(d).wait_recv())
    xall[c, t] = dot(packing, z_recv[...].reshape(128, PART)).astype(BF)

    def x1_copy(j):
        return remote(
            xall.at[c, t], xall.at[c, t], x1_ss.at[j], x1_rs.at[j], (b, place(c, g, wrap(m + j, 4)))
        )

    def x2_copy(j, d):
        s = place(c, g, wrap(m - j, 4))
        n = 4 * j + d
        return remote(
            xall.at[c, s], xall.at[c, s], x2_ss.at[n], x2_rs.at[n], (b, place(c, wrap(g + d, 4), m))
        )

    def xp_copy(j, d):
        s = place(c, wrap(g - d, 4), wrap(m - j, 4))
        n = 4 * j + d
        return remote(xall.at[c, s], xall.at[c, s], xp_ss.at[n], xp_rs.at[n], (partner, t))

    loop(1, 4, lambda j: x1_copy(j).start())
    loop(1, 4, lambda d: x2_copy(0, d).start())
    xp_copy(0, 0).start()

    def pass_on(j):
        x1_copy(j).wait_recv()
        loop(1, 4, lambda d: x2_copy(j, d).start())
        xp_copy(j, 0).start()

    loop(1, 4, pass_on)

    def multiply(core, side, s):
        rows = xall[core, s]
        cols = pl.ds(pl.multiple_of(s * PART, 128), PART)
        acc[side, 0] += dot(rows, win[0, :, cols], NT)
        acc[side, 1] += dot(rows, win[1, :, cols], NT)
        plain = rows.astype(F32) * (1.0 / gain_ref[:, cols])
        plain = plain * plain
        vacc[side] += plain[:, 0:128] + plain[:, 128:256] + plain[:, 256:384]

    def own_slice(n):
        d, j = lax.div(n, 4), lax.rem(n, 4)
        multiply(c, 0, place(c, wrap(g - d, 4), wrap(m - j, 4)))

    def partner_slice(n):
        d, j = lax.div(n, 4), lax.rem(n, 4)
        xp_copy(j, d).wait_recv()
        multiply(1 - c, 1, place(1 - c, wrap(m - d, 4), wrap(g - j, 4)))

    def gather_step(n):
        d, j = lax.div(n, 4), lax.rem(n, 4)
        x2_copy(j, d).wait_recv()
        xp_copy(j, d).start()
        own_slice(n)
        partner_slice(n - 4)

    loop(0, 4, own_slice)
    loop(4, 16, gather_step)
    loop(12, 16, partner_slice)

    for side in range(2):
        spread2 = jnp.sum(vacc[side], axis=1, keepdims=True) * (1.0 / D)
        inverse = lax.rsqrt(spread2 + EPS)
        gate, up = acc[side, 0] * inverse, acc[side, 1] * inverse
        hid[side] = (gate / (1.0 + jnp.exp(-gate)) * up).astype(BF)

    def slab(side, s):
        return dot(hid[side], wdn[:, pl.ds(pl.multiple_of(s * PART, 128), PART)])

    def q_copy(n):
        return remote(q_send.at[n], q_recv.at[n], q_ss.at[n], q_rs.at[n], (partner, t))

    def for_partner(n):
        d, j = 1 + lax.div(n, 4), lax.rem(n, 4)
        q_send[n] = slab(1, place(1 - c, wrap(m + d, 4), wrap(g + j, 4))).astype(BF)
        q_copy(n).start()

    def chip_sum(n):
        d, j = 1 + lax.div(n, 4), lax.rem(n, 4)
        own = slab(0, place(c, wrap(g + d, 4), wrap(m + j, 4)))
        q_copy(n).wait_recv()
        return own + q_recv[n].astype(F32)

    def g_copy(n):
        d = 1 + lax.div(n, 4)
        return remote(
            g_send.at[n], g_recv.at[n], g_ss.at[n], g_rs.at[n], (b, place(c, wrap(g + d, 4), m))
        )

    def down_step(n):
        for_partner(n)
        g_send[n - 4] = chip_sum(n - 4).astype(BF)
        g_copy(n - 4).start()

    def keep_step(n):
        chip[n - 12] = chip_sum(n)

    loop(0, 4, for_partner)
    loop(4, 16, down_step)
    loop(12, 16, keep_step)

    def m_copy(j):
        return remote(
            m_send.at[j], m_recv.at[j], m_ss.at[j], m_rs.at[j], (b, place(c, g, wrap(m + j, 4)))
        )

    def group_sum(j):
        for d in range(3):
            g_copy(4 * d + j).wait_recv()
        return (
            chip[j] + g_recv[j].astype(F32) + g_recv[4 + j].astype(F32) + g_recv[8 + j].astype(F32)
        )

    def member_step(j):
        m_send[j] = group_sum(j).astype(BF)
        m_copy(j).start()

    loop(1, 4, member_step)
    final = group_sum(0)
    loop(1, 4, lambda j: m_copy(j).wait_recv())
    for j in range(1, 4):
        final = final + m_recv[j].astype(F32)

    y_send[...] = dot(packing, final.astype(BF), TN).astype(BF).reshape(EXPERTS, 16, PART)
    y_recv[z] = y_send[z]

    def y_copy(d):
        to = wrap(z + d, 8)
        return remote(y_send.at[to], y_recv.at[z], y_ss.at[d], y_rs.at[d], (2 * to + c, t))

    loop(1, 8, lambda d: y_copy(d).start())

    loop(1, 16, lambda i: a_copy(i).wait_send())
    loop(1, 16, lambda i: b_copy(i).wait_send())
    loop(1, 8, lambda d: z_copy(d).wait_send())
    loop(1, 4, lambda j: x1_copy(j).wait_send())
    loop(0, 4, lambda j: loop(1, 4, lambda d: x2_copy(j, d).wait_send()))
    loop(0, 16, lambda n: xp_copy(lax.div(n, 4), lax.rem(n, 4)).wait_send())
    loop(0, 16, lambda n: q_copy(n).wait_send())
    loop(0, 12, lambda n: g_copy(n).wait_send())
    loop(1, 4, lambda j: m_copy(j).wait_send())

    loop(1, 8, lambda d: y_copy(d).wait_recv())
    returned = y_recv[...].reshape(128, PART)
    mix = dot(combine_high, returned) + dot(combine_low, returned)
    out_ref[...] = (state[...] + mix).astype(BF)
    loop(1, 8, lambda d: y_copy(d).wait_send())


def body(queries, new_kv, cache, residual, w_out, norm_gain, routes, route_weight, w_in, w_down):
    heads = queries.reshape(ROWS, STEPS, 16, 3, HD).transpose(0, 2, 3, 1, 4)
    heads = heads.reshape(ROWS, 16, 6, HD)
    heads = jnp.pad(heads, ((0, 0), (0, 0), (0, 2), (0, 0))).reshape(ROWS, 128, HD)
    fresh = new_kv.reshape(2, ROWS, STEPS, KV, HD).transpose(0, 1, 3, 2, 4)
    fresh = fresh.reshape(2, ROWS, 16, HD)
    stream = jnp.pad(residual.reshape(12, D), ((0, 4), (0, 0)))
    chosen = jnp.pad(routes.reshape(12, TOP), ((0, 4), (0, 0)), constant_values=-1)
    factors = jnp.pad(route_weight.reshape(12, TOP), ((0, 4), (0, 0)))
    w_in_t = w_in.transpose(0, 2, 3, 1).reshape(2, UNITS, D)
    w_down = w_down.reshape(UNITS, D)
    gain = norm_gain.reshape(1, D)
    vmem = pl.BlockSpec(memory_space=pltpu.VMEM)
    hbm = pl.BlockSpec(memory_space=pl.ANY)
    dma = pltpu.SemaphoreType.DMA
    out = pl.pallas_call(
        kernel,
        out_shape=jax.ShapeDtypeStruct((16, PART), BF),
        in_specs=[vmem, vmem, hbm, vmem, hbm, vmem, vmem, vmem, hbm, hbm],
        out_specs=vmem,
        scratch_shapes=[
            pltpu.VMEM((2, ROWS, KV, KEYS, HD), BF),
            pltpu.VMEM((PART, D), BF),
            pltpu.VMEM((2, UNITS, D), BF),
            pltpu.VMEM((UNITS, D), BF),
            pltpu.VMEM((16, 64, 128), BF),
            pltpu.VMEM((16, 64, 128), BF),
            pltpu.VMEM((128, 128), F32),
            pltpu.VMEM((128, 128), F32),
            pltpu.VMEM((16, PART), F32),
            pltpu.VMEM((16, 16, PART), F32),
            pltpu.VMEM((16, 16, PART), BF),
            pltpu.VMEM((16, 16, PART), BF),
            pltpu.VMEM((16, PART), F32),
            pltpu.VMEM((EXPERTS, 16, PART), BF),
            pltpu.VMEM((EXPERTS, 16, PART), BF),
            pltpu.VMEM((2, 16, PACK, PART), BF),
            pltpu.VMEM((2, 2, PACK, UNITS), F32),
            pltpu.VMEM((2, PACK, 128), F32),
            pltpu.VMEM((2, PACK, UNITS), BF),
            pltpu.VMEM((16, PACK, PART), BF),
            pltpu.VMEM((16, PACK, PART), BF),
            pltpu.VMEM((12, PACK, PART), BF),
            pltpu.VMEM((12, PACK, PART), BF),
            pltpu.VMEM((4, PACK, PART), F32),
            pltpu.VMEM((4, PACK, PART), BF),
            pltpu.VMEM((4, PACK, PART), BF),
            pltpu.VMEM((EXPERTS, 16, PART), BF),
            pltpu.VMEM((EXPERTS, 16, PART), BF),
            dma((2, ROWS)),
            dma((3,)),
            dma((16,)), dma((16,)),
            dma((16,)), dma((16,)),
            dma((8,)), dma((8,)),
            dma((4,)), dma((4,)),
            dma((16,)), dma((16,)),
            dma((16,)), dma((16,)),
            dma((16,)), dma((16,)),
            dma((12,)), dma((12,)),
            dma((4,)), dma((4,)),
            dma((8,)), dma((8,)),
        ],
        compiler_params=pltpu.CompilerParams(
            collective_id=0, has_side_effects=True, vmem_limit_bytes=48 * 1024 * 1024
        ),
        name="layer",
    )(heads, fresh, cache, stream, w_out, gain, chosen, factors, w_in_t, w_down)
    return out[:12].reshape(ROWS, STEPS, PART)


def solution(mesh):
    return jax.shard_map(
        body,
        mesh=mesh,
        in_specs=(
            P("expert", None, None),
            P(None, "expert", None, None),
            P(None, "expert", None, "tensor", None),
            P("expert", None, None),
            P("tensor", None),
            P(),
            P("expert", None, None),
            P("expert", None, None),
            P("expert", None, None, "tensor"),
            P("expert", "tensor", None),
        ),
        out_specs=P("expert", None, "tensor"),
        check_vma=False,
    )
```

```python
import jax
import jax.numpy as jnp
from jax import lax
from jax.experimental import pallas as pl
from jax.experimental.pallas import tpu as pltpu
from jax.sharding import PartitionSpec as P

D = 6144
HEADS = 48
KV = 8
HD = 128
EXPERTS = 8
TOP = 4
CAP = 9
ROWS = 6
STEPS = 2
KEYS = 256
UNITS = 168
PART = 384
PACK = 80
EPS = 1e-05
BF = jnp.bfloat16
F32 = jnp.float32
MESH = pl.DeviceIdType.MESH
NT = (((1,), (1,)), ((), ()))
FAR_Z = (4, 3, 5, 2, 6, 1, 7)
FAR_PLANE = (10, 6, 9, 11, 14, 2, 8, 5, 7, 13, 15, 1, 3, 4, 12)
FAR_RING = (2, 1, 3)
MEMBERS = (2, 1, 3, 0)


def wrap(value, size):
    return lax.rem(value + size, size)


def iota(shape, dim):
    return lax.broadcasted_iota(jnp.int32, shape, dim)


def dot(a, b, dims=None):
    if dims is None:
        return jnp.dot(a, b, preferred_element_type=F32)
    return lax.dot_general(a, b, dims, preferred_element_type=F32)


def kernel(
    q_hbm, nkv_hbm, cache_hbm, res_hbm, wout_hbm, gain_hbm, routes_hbm, rw_hbm, win_hbm, wdn_hbm,
    out_ref,
    q_raw, nkv, res_raw, gain_ref, routes_raw, rw_raw, q_ref, res, choice,
    kv, wout, win, wdn,
    a_send, a_recv, stat, fcol, att, proj, b_send, b_recv,
    state, z_send, z_recv, xall, acc, vacc, hid,
    own, q_send, q_recv, g_send, g_recv, chip, m_send, m_recv, y_send, y_recv,
    in_sem, kv_sem, w_sem,
    a_ss, a_rs, b_ss, b_rs, z_ss, z_rs, x1_ss, x1_rs, x2_ss, x2_rs, xp_ss, xp_rs,
    q_ss, q_rs, g_ss, g_rs, m_ss, m_rs, y_ss, y_rs,
):
    b = lax.axis_index("expert")
    t = lax.axis_index("tensor")
    z, c = lax.div(b, 2), lax.rem(b, 2)
    y, x = lax.div(t, 4), lax.rem(t, 4)
    partner = 2 * z + 1 - c
    m = (1 - c) * x + c * y
    g = (1 - c) * y + c * x

    def place(core, group, member):
        return (1 - core) * (4 * group + member) + core * (4 * member + group)

    def plane_peer(i):
        return 4 * wrap(y + i // 4, 4) + wrap(x + i % 4, 4)

    def remote(src, dst, ss, rs, dev):
        return pltpu.make_async_remote_copy(
            src_ref=src, dst_ref=dst, send_sem=ss, recv_sem=rs, device_id=dev, device_id_type=MESH
        )

    inputs = [
        pltpu.make_async_copy(src, dst, in_sem.at[i])
        for i, (src, dst) in enumerate(
            [
                (q_hbm, q_raw), (nkv_hbm, nkv), (res_hbm, res_raw), (gain_hbm, gain_ref),
                (routes_hbm, routes_raw), (rw_hbm, rw_raw),
            ]
        )
    ]
    rows_in = [
        [
            pltpu.make_async_copy(cache_hbm.at[s, r], kv.at[s, r], kv_sem.at[s, r])
            for s in range(2)
        ]
        for r in range(ROWS)
    ]
    weights_in = [
        pltpu.make_async_copy(wout_hbm, wout, w_sem.at[0]),
        pltpu.make_async_copy(win_hbm, win, w_sem.at[1]),
        pltpu.make_async_copy(wdn_hbm, wdn, w_sem.at[2]),
    ]
    inputs[0].start()
    inputs[1].start()
    for pair in rows_in:
        for copy in pair:
            copy.start()
    for copy in inputs[2:]:
        copy.start()

    barrier = pltpu.get_barrier_semaphore()

    def greet(dev):
        pl.semaphore_signal(barrier, inc=1, device_id=dev, device_id_type=MESH)

    for d in FAR_Z:
        greet((2 * wrap(z + d, 8) + c, t))
    for i in FAR_PLANE:
        greet((b, plane_peer(i)))
    greet((partner, t))

    inputs[0].wait()
    nothing = jnp.zeros((2, HD), F32)
    for r in range(ROWS):
        both = q_raw[r].astype(F32)
        pieces = []
        for owner in range(16):
            for h in range(3):
                lo = HD * (3 * owner + h)
                pieces.append(both[:, lo : lo + HD])
            pieces.append(nothing)
        q_ref[r] = jnp.concatenate(pieces, axis=0).astype(BF)
    inputs[1].wait()

    row_id = iota((128, 16), 0)
    key_id = iota((128, 16), 1)
    fresh_ok = (
        (lax.div(row_id, 16) == lax.div(key_id, 2))
        & (lax.rem(key_id, 2) <= lax.rem(row_id, 2))
        & (jnp.broadcast_to(t, (128, 16)) == 0)
    )
    lane = iota((128, 128), 1)
    tallies = jnp.zeros((128, 128), F32)
    for pair in range(3):
        if pair == 2:
            weights_in[0].start()
        halves = []
        for r in (2 * pair, 2 * pair + 1):
            rows_in[r][0].wait()
            qr = q_ref[r]
            scores = jnp.concatenate(
                [dot(qr[16 * k : 16 * k + 16], kv[0, r, k], NT) for k in range(KV)], axis=0
            ) * (HD**-0.5)
            extra = dot(qr, nkv[0, r], NT) * (HD**-0.5)
            extra = jnp.where(fresh_ok, extra, -jnp.inf)
            top = jnp.maximum(
                jnp.max(scores, axis=1, keepdims=True), jnp.max(extra, axis=1, keepdims=True)
            )
            top = jnp.ceil(top * 0.25) * 4.0
            weights = jnp.exp(scores - top)
            extra = jnp.exp(extra - top)
            total = jnp.sum(weights, axis=1, keepdims=True) + jnp.sum(extra, axis=1, keepdims=True)
            low = weights.astype(BF)
            rows_in[r][1].wait()
            mixed = jnp.concatenate(
                [dot(low[16 * k : 16 * k + 16], kv[1, r, k]) for k in range(KV)], axis=0
            ) + dot(extra.astype(BF), nkv[1, r])
            tallies = jnp.where(lane == r, top, jnp.where(lane == 8 + r, total, tallies))
            halves.append(mixed.reshape(16, 8, 128))
        a_send[:, 16 * pair : 16 * pair + 16, :] = jnp.concatenate(halves, axis=1).astype(BF)
    table = jnp.transpose(tallies)[0:16, :].astype(BF)
    a_send[:, 48:64, :] = jnp.broadcast_to(table[None], (16, 16, 128))
    pl.semaphore_wait(barrier, 23)

    def a_copy(i):
        to = plane_peer(i)
        return remote(a_send.at[to], a_recv.at[t], a_ss.at[i], a_rs.at[i], (b, to))

    for i in FAR_PLANE:
        a_copy(i).start()
    a_recv[t] = a_send[t]
    weights_in[1].start()
    weights_in[2].start()

    for copy in inputs[2:]:
        copy.wait()
    choice[...] = jnp.zeros_like(choice)
    for s in range(STEPS):
        choice[4 * s : 4 * s + 4, 0:ROWS] = routes_raw[s].astype(F32) + 1.0
        choice[8 + 4 * s : 12 + 4 * s, 0:ROWS] = rw_raw[s]
    turned = jnp.transpose(choice[...])
    slot_lane = iota((16, 128), 1)
    token_row = iota((16, 128), 0)
    lane_expert = lax.div(slot_lane, 16).astype(F32) + 1.0
    chosen = jnp.zeros((16, 128), F32)
    factor = jnp.zeros((16, 128), F32)
    for k in range(TOP):
        named = jnp.concatenate([turned[0:8, k : k + 1], turned[0:8, 4 + k : 5 + k]], axis=0)
        amount = jnp.concatenate([turned[0:8, 8 + k : 9 + k], turned[0:8, 12 + k : 13 + k]], axis=0)
        hit = named == lane_expert
        chosen = jnp.where(hit, 1.0, chosen)
        factor = jnp.where(hit, amount, factor)
    below = (iota((16, 16), 1) < iota((16, 16), 0)).astype(BF)
    earlier = dot(below, chosen.astype(BF))
    here = (chosen > 0.5) & (earlier.astype(jnp.int32) == lax.rem(slot_lane, 16))
    dispatch = jnp.transpose(
        jnp.concatenate([jnp.where(here, 1.0, 0.0), jnp.zeros((112, 128), F32)], axis=0)
    )[:, 0:16].astype(BF)
    combine = jnp.where(here, factor, 0.0)
    combine_high = combine.astype(BF)
    combine_low = (combine - combine_high.astype(F32)).astype(BF)
    mine = pl.ds(pl.multiple_of(t * PART, 128), PART)
    res[...] = jnp.zeros_like(res)
    for r in range(ROWS):
        both = res_raw[r].astype(F32)
        res[r : r + 1, :] = both[0:1]
        res[8 + r : 9 + r, :] = both[1:2]
    res_sum = jnp.sum(res[...], axis=1, keepdims=True)
    res_mine = res[:, mine]
    gain_mine = gain_ref[:, mine]

    def slots(row, slot):
        rank = lax.rem(slot, 16)
        return jnp.where((row == CAP * lax.div(slot, 16) + rank) & (rank < CAP), 1.0, 0.0).astype(BF)

    packing = slots(iota((PACK, 128), 0), iota((PACK, 128), 1))
    unpacking = slots(iota((128, PACK), 1), iota((128, PACK), 0))
    acc[...] = jnp.zeros_like(acc)
    vacc[...] = jnp.zeros_like(vacc)
    att[...] = jnp.zeros_like(att)
    weights_in[0].wait()

    for i in reversed(FAR_PLANE):
        a_copy(i).wait_recv()

    stats = a_recv[:, 48:64, :].astype(F32)
    tops, totals = stats[:, 0:8], stats[:, 8:16]
    top = jnp.max(tops, axis=0, keepdims=True)
    scale = jnp.exp(tops - top)
    whole = jnp.sum(scale * totals, axis=0, keepdims=True)
    scale = scale / jnp.maximum(whole, 1e-30)
    fcol[...] = jnp.transpose(scale.reshape(128, 128))
    columns = fcol[pl.ds(pl.multiple_of(8 * t, 8), 8), :]
    for pair in range(3):
        both = a_recv[:, 16 * pair : 16 * pair + 16, :].astype(F32)
        for half in range(2):
            r = 2 * pair + half
            joined = jnp.zeros((8, 128), F32)
            for s in range(16):
                joined += both[s, 8 * half : 8 * half + 8] * columns[:, 8 * s + r : 8 * s + r + 1]
            for h in range(3):
                for s in range(STEPS):
                    att[8 * s + r : 8 * s + r + 1, 128 * h : 128 * h + 128] = joined[
                        2 * h + s : 2 * h + s + 1
                    ]

    attended = att[...].astype(BF)
    proj_sum = jnp.zeros((16, 1), F32)
    for s in range(16):
        part = dot(attended, wout[:, PART * s : PART * s + PART])
        proj[s] = part
        proj_sum = proj_sum + jnp.sum(part, axis=1, keepdims=True)
    diagonal = jnp.sum(jnp.where(token_row == slot_lane, proj_sum, 0.0), axis=0, keepdims=True)
    high = diagonal.astype(BF).astype(F32)
    low = diagonal - high
    head = jnp.where(token_row == 6, high, jnp.where(token_row == 7, low, 0.0))
    head = jnp.concatenate([head, jnp.zeros((16, PART - 128), F32)], axis=1)

    def b_copy(i):
        to = plane_peer(i)
        return remote(b_send.at[to], b_recv.at[t], b_ss.at[i], b_rs.at[i], (b, to))

    for i in FAR_PLANE:
        to = plane_peer(i)
        b_send[to] = (proj[to] + head).astype(BF)
        b_copy(i).start()
    b_recv[t] = (proj[t] + head).astype(BF)
    for i in reversed(FAR_PLANE):
        b_copy(i).wait_recv()

    summed = jnp.sum(b_recv[...].astype(F32), axis=0)
    spread = jnp.where(token_row == slot_lane, summed[6:7, 0:128] + summed[7:8, 0:128], 0.0)
    mean = (jnp.sum(spread, axis=1, keepdims=True) + res_sum) * (1.0 / D)
    real = lax.rem(iota((16, PART), 0), 8) < ROWS
    hidden = jnp.where(real, summed + res_mine, 0.0)
    state[...] = hidden
    scaled = jnp.where(real, (hidden - mean) * gain_mine, 0.0).astype(BF)

    z_send[...] = dot(dispatch, scaled).astype(BF).reshape(EXPERTS, 16, PART)

    def z_copy(d):
        to = wrap(z + d, 8)
        return remote(z_send.at[to], z_recv.at[z], z_ss.at[d], z_rs.at[d], (2 * to + c, t))

    for d in FAR_Z:
        z_copy(d).start()
    z_recv[z] = z_send[z]
    weights_in[1].wait()
    weights_in[2].wait()
    for d in reversed(FAR_Z):
        z_copy(d).wait_recv()
    xall[c, t] = dot(packing, z_recv[...].reshape(128, PART)).astype(BF)

    def x1_copy(j):
        return remote(
            xall.at[c, t], xall.at[c, t], x1_ss.at[j], x1_rs.at[j], (b, place(c, g, wrap(m + j, 4)))
        )

    def x2_copy(j, d):
        s = place(c, g, wrap(m - j, 4))
        n = 4 * j + d
        return remote(
            xall.at[c, s], xall.at[c, s], x2_ss.at[n], x2_rs.at[n], (b, place(c, wrap(g + d, 4), m))
        )

    def xp_copy(j, d):
        s = place(c, wrap(g - d, 4), wrap(m - j, 4))
        n = 4 * j + d
        return remote(xall.at[c, s], xall.at[c, s], xp_ss.at[n], xp_rs.at[n], (partner, t))

    def multiply(core, side, found):
        rows = jnp.concatenate([xall[core, s] for s in found], axis=1)
        cols = [pl.ds(pl.multiple_of(s * PART, 128), PART) for s in found]
        for u in range(2):
            units = jnp.concatenate([win[u, :, col] for col in cols], axis=1)
            acc[side, u] += dot(rows, units, NT)
        squares = vacc[side]
        for s, col in zip(found, cols):
            plain = xall[core, s].astype(F32) * (1.0 / gain_ref[:, col])
            plain = plain * plain
            squares += plain[:, 0:128] + plain[:, 128:256] + plain[:, 256:384]
        vacc[side] = squares

    def own_part(j):
        for d in FAR_RING:
            x2_copy(j, d).wait_recv()
            xp_copy(j, d).start()

    def own_multiply(j):
        multiply(c, 0, [place(c, wrap(g - d, 4), wrap(m - j, 4)) for d in range(4)])

    def partner_multiply(j):
        for d in range(4):
            xp_copy(j, d).wait_recv()
        multiply(1 - c, 1, [place(1 - c, wrap(m - d, 4), wrap(g - j, 4)) for d in range(4)])

    for j in FAR_RING:
        x1_copy(j).start()
    for d in FAR_RING:
        x2_copy(0, d).start()
    xp_copy(0, 0).start()
    for j in (1, 3, 2):
        x1_copy(j).wait_recv()
        for d in FAR_RING:
            x2_copy(j, d).start()
        xp_copy(j, 0).start()
    own_part(0)
    own_multiply(0)
    own_part(1)
    own_multiply(1)
    partner_multiply(0)
    own_part(3)
    own_multiply(3)
    partner_multiply(1)
    own_part(2)
    partner_multiply(3)
    own_multiply(2)
    partner_multiply(2)

    for side in range(2):
        inverse = lax.rsqrt(jnp.sum(vacc[side], axis=1, keepdims=True) * (1.0 / D) + EPS)
        gate, up = acc[side, 0] * inverse, acc[side, 1] * inverse
        hid[PACK * side : PACK * side + PACK] = (gate / (1.0 + jnp.exp(-gate)) * up).astype(BF)

    def q_copy(n):
        part = pl.ds(4 * n, 4)
        return remote(q_send.at[part], q_recv.at[part], q_ss.at[n], q_rs.at[n], (partner, t))

    for n in range(4):
        slab = dot(hid[...], wdn[:, 4 * PART * n : 4 * PART * n + 4 * PART])
        for i in range(4):
            q_send[4 * n + i] = slab[PACK:, PART * i : PART * i + PART].astype(BF)
        q_copy(n).start()
        for i in range(4):
            own[4 * n + i] = slab[:PACK, PART * i : PART * i + PART]

    def g_copy(j, d):
        n = 3 * j + d - 1
        return remote(
            g_send.at[n], g_recv.at[n], g_ss.at[n], g_rs.at[n], (b, place(c, wrap(g + d, 4), m))
        )

    def m_copy(j):
        return remote(
            m_send.at[j], m_recv.at[j], m_ss.at[j], m_rs.at[j], (b, place(c, g, wrap(m + j, 4)))
        )

    for n in range(4):
        q_copy(n).wait_recv()
    for j in MEMBERS:
        for d in FAR_RING:
            s = place(c, wrap(g + d, 4), wrap(m + j, 4))
            g_send[3 * j + d - 1] = (own[s] + q_recv[s].astype(F32)).astype(BF)
            g_copy(j, d).start()
        s = place(c, g, wrap(m + j, 4))
        chip[j] = own[s] + q_recv[s].astype(F32)

    final = None
    for j in MEMBERS:
        whole = chip[j]
        for d in FAR_RING:
            g_copy(j, d).wait_recv()
            whole = whole + g_recv[3 * j + d - 1].astype(F32)
        if j:
            m_send[j] = whole.astype(BF)
            m_copy(j).start()
        else:
            final = whole
    for j in (1, 3, 2):
        m_copy(j).wait_recv()
        final = final + m_recv[j].astype(F32)

    y_send[...] = dot(unpacking, final.astype(BF)).astype(BF).reshape(EXPERTS, 16, PART)

    def y_copy(d):
        to = wrap(z + d, 8)
        return remote(y_send.at[to], y_recv.at[z], y_ss.at[d], y_rs.at[d], (2 * to + c, t))

    for d in FAR_Z:
        y_copy(d).start()
    y_recv[z] = y_send[z]

    for i in FAR_PLANE:
        a_copy(i).wait_send()
        b_copy(i).wait_send()
    for d in FAR_Z:
        z_copy(d).wait_send()
    for j in FAR_RING:
        x1_copy(j).wait_send()
        m_copy(j).wait_send()
    for j in range(4):
        q_copy(j).wait_send()
        for d in range(4):
            xp_copy(j, d).wait_send()
        for d in FAR_RING:
            x2_copy(j, d).wait_send()
            g_copy(j, d).wait_send()

    for d in reversed(FAR_Z):
        y_copy(d).wait_recv()
    returned = y_recv[...].reshape(128, PART)
    mix = dot(combine_high, returned) + dot(combine_low, returned)
    mixed = state[...] + mix
    for r in range(ROWS):
        out_ref[r] = jnp.concatenate([mixed[r : r + 1], mixed[8 + r : 9 + r]], axis=0).astype(BF)
    for d in FAR_Z:
        y_copy(d).wait_send()


def body(queries, new_kv, cache, residual, w_out, norm_gain, routes, route_weight, w_in, w_down):
    fresh = new_kv.reshape(2, ROWS, STEPS, KV, HD).transpose(0, 1, 3, 2, 4)
    fresh = fresh.reshape(2, ROWS, 16, HD)
    w_in_t = w_in.transpose(0, 2, 3, 1).reshape(2, UNITS, D)
    w_down = w_down.reshape(UNITS, D)
    gain = norm_gain.reshape(1, D)
    chosen = routes.transpose(1, 2, 0)
    factors = route_weight.transpose(1, 2, 0)
    hbm = pl.BlockSpec(memory_space=pltpu.HBM)
    dma = pltpu.SemaphoreType.DMA
    vmem = pltpu.VMEM
    return pl.pallas_call(
        kernel,
        out_shape=jax.ShapeDtypeStruct((ROWS, STEPS, PART), BF),
        in_specs=[hbm] * 10,
        out_specs=pl.BlockSpec(memory_space=pltpu.VMEM),
        scratch_shapes=[
            vmem((ROWS, STEPS, D), BF),
            vmem((2, ROWS, 16, HD), BF),
            vmem((ROWS, STEPS, D), BF),
            vmem((1, D), F32),
            vmem((STEPS, TOP, ROWS), jnp.int32),
            vmem((STEPS, TOP, ROWS), F32),
            vmem((ROWS, 128, HD), BF),
            vmem((16, D), F32),
            vmem((128, 128), F32),
            vmem((2, ROWS, KV, KEYS, HD), BF),
            vmem((PART, D), BF),
            vmem((2, UNITS, D), BF),
            vmem((UNITS, D), BF),
            vmem((16, 64, 128), BF),
            vmem((16, 64, 128), BF),
            vmem((128, 128), F32),
            vmem((128, 128), F32),
            vmem((16, PART), F32),
            vmem((16, 16, PART), F32),
            vmem((16, 16, PART), BF),
            vmem((16, 16, PART), BF),
            vmem((16, PART), F32),
            vmem((EXPERTS, 16, PART), BF),
            vmem((EXPERTS, 16, PART), BF),
            vmem((2, 16, PACK, PART), BF),
            vmem((2, 2, PACK, UNITS), F32),
            vmem((2, PACK, 128), F32),
            vmem((2 * PACK, UNITS), BF),
            vmem((16, PACK, PART), F32),
            vmem((16, PACK, PART), BF),
            vmem((16, PACK, PART), BF),
            vmem((12, PACK, PART), BF),
            vmem((12, PACK, PART), BF),
            vmem((4, PACK, PART), F32),
            vmem((4, PACK, PART), BF),
            vmem((4, PACK, PART), BF),
            vmem((EXPERTS, 16, PART), BF),
            vmem((EXPERTS, 16, PART), BF),
            dma((6,)),
            dma((2, ROWS)),
            dma((3,)),
            dma((16,)), dma((16,)),
            dma((16,)), dma((16,)),
            dma((8,)), dma((8,)),
            dma((4,)), dma((4,)),
            dma((16,)), dma((16,)),
            dma((16,)), dma((16,)),
            dma((4,)), dma((4,)),
            dma((12,)), dma((12,)),
            dma((4,)), dma((4,)),
            dma((8,)), dma((8,)),
        ],
        compiler_params=pltpu.CompilerParams(
            collective_id=0, has_side_effects=True, vmem_limit_bytes=56 * 1024 * 1024
        ),
        name="layer",
    )(queries, fresh, cache, residual, w_out, gain, chosen, factors, w_in_t, w_down)


def solution(mesh):
    return jax.shard_map(
        body,
        mesh=mesh,
        in_specs=(
            P("expert", None, None),
            P(None, "expert", None, None),
            P(None, "expert", None, "tensor", None),
            P("expert", None, None),
            P("tensor", None),
            P(),
            P("expert", None, None),
            P("expert", None, None),
            P("expert", None, None, "tensor"),
            P("expert", "tensor", None),
        ),
        out_specs=P("expert", None, "tensor"),
        check_vma=False,
    )
```

```python
import jax
import jax.numpy as jnp
from jax import lax
from jax.experimental import pallas as pl
from jax.experimental.pallas import tpu as pltpu
from jax.sharding import PartitionSpec as P

D = 6144
HEADS = 48
KV = 8
HD = 128
EXPERTS = 8
TOP = 4
CAP = 9
ROWS = 6
STEPS = 2
KEYS = 256
UNITS = 168
PART = 384
PACK = 80
EPS = 1e-05
BF = jnp.bfloat16
F32 = jnp.float32
MESH = pl.DeviceIdType.MESH
NT = (((1,), (1,)), ((), ()))
FAR_Z = (4, 3, 5, 2, 6, 1, 7)
FAR_PLANE = (10, 6, 9, 11, 14, 2, 8, 5, 7, 13, 15, 1, 3, 4, 12)
FAR_RING = (2, 1, 3)
ORDER = (0, 1, 7, 2, 6, 3, 5, 4)
NEAR = 5
GROUPS = ((0, 48), (48, 32))
MEMBERS = (2, 1, 3, 0)


def wrap(value, size):
    return lax.rem(value + size, size)


def iota(shape, dim):
    return lax.broadcasted_iota(jnp.int32, shape, dim)


def dot(a, b, dims=None):
    if dims is None:
        return jnp.dot(a, b, preferred_element_type=F32)
    return lax.dot_general(a, b, dims, preferred_element_type=F32)


def kernel(
    q_hbm, nkv_hbm, cache_hbm, res_hbm, wout_hbm, gain_hbm, routes_hbm, rw_hbm, win_hbm, wdn_hbm,
    out_ref,
    q_raw, nkv, res_raw, gain_ref, routes_raw, rw_raw, q_ref, res, choice, ordered,
    kv, wout, win, wdn,
    a_send, a_recv, stat, fcol, att, proj, b_send, b_recv,
    state, z_send, z_recv, xall, acc, vacc, hid,
    own, q_send, q_recv, g_send, g_recv, m_send, m_recv, y_send, y_recv,
    in_sem, kv_sem, w_sem,
    a_ss, a_rs, b_ss, b_rs, z_ss, z_rs, x1_ss, x1_rs, x2_ss, x2_rs, xp_ss, xp_rs,
    q_ss, q_rs, g_ss, g_rs, m_ss, m_rs, y_ss, y_rs,
):
    b = lax.axis_index("expert")
    t = lax.axis_index("tensor")
    z, c = lax.div(b, 2), lax.rem(b, 2)
    y, x = lax.div(t, 4), lax.rem(t, 4)
    partner = 2 * z + 1 - c
    m = (1 - c) * x + c * y
    g = (1 - c) * y + c * x

    def place(core, group, member):
        return (1 - core) * (4 * group + member) + core * (4 * member + group)

    def plane_peer(i):
        return 4 * wrap(y + i // 4, 4) + wrap(x + i % 4, 4)

    def remote(src, dst, ss, rs, dev):
        return pltpu.make_async_remote_copy(
            src_ref=src, dst_ref=dst, send_sem=ss, recv_sem=rs, device_id=dev, device_id_type=MESH
        )

    inputs = [
        pltpu.make_async_copy(src, dst, in_sem.at[i])
        for i, (src, dst) in enumerate(
            [
                (q_hbm, q_raw), (nkv_hbm, nkv), (res_hbm, res_raw), (gain_hbm, gain_ref),
                (routes_hbm, routes_raw), (rw_hbm, rw_raw),
            ]
        )
    ]
    rows_in = [
        [
            pltpu.make_async_copy(cache_hbm.at[s, r], kv.at[s, r], kv_sem.at[s, r])
            for s in range(2)
        ]
        for r in range(ROWS)
    ]
    weights_in = [
        pltpu.make_async_copy(wout_hbm, wout, w_sem.at[0]),
        pltpu.make_async_copy(win_hbm, win, w_sem.at[1]),
        pltpu.make_async_copy(wdn_hbm, wdn, w_sem.at[2]),
    ]
    inputs[0].start()
    inputs[1].start()
    for pair in rows_in[:3]:
        for copy in pair:
            copy.start()

    barrier = pltpu.get_barrier_semaphore()

    def greet(dev):
        pl.semaphore_signal(barrier, inc=1, device_id=dev, device_id_type=MESH)

    for d in FAR_Z:
        greet((2 * wrap(z + d, 8) + c, t))
    for i in FAR_PLANE:
        greet((b, plane_peer(i)))
    greet((partner, t))

    inputs[0].wait()
    nothing = jnp.zeros((2, HD), F32)
    for r in range(ROWS):
        both = q_raw[r].astype(F32)
        pieces = []
        for owner in range(16):
            for h in range(3):
                lo = HD * (3 * owner + h)
                pieces.append(both[:, lo : lo + HD])
            pieces.append(nothing)
        q_ref[r] = jnp.concatenate(pieces, axis=0).astype(BF)
    inputs[1].wait()

    row_id = iota((128, 16), 0)
    key_id = iota((128, 16), 1)
    fresh_ok = (
        (lax.div(row_id, 16) == lax.div(key_id, 2))
        & (lax.rem(key_id, 2) <= lax.rem(row_id, 2))
        & (jnp.broadcast_to(t, (128, 16)) == 0)
    )
    lane = iota((128, 128), 1)
    tallies = jnp.zeros((128, 128), F32)
    for pair in range(3):
        halves = []
        for r in (2 * pair, 2 * pair + 1):
            rows_in[r][0].wait()
            if r + 3 < ROWS:
                for copy in rows_in[r + 3]:
                    copy.start()
            if r == 3:
                for copy in inputs[2:] + weights_in[:1]:
                    copy.start()
            qr = q_ref[r]
            scores = jnp.concatenate(
                [dot(qr[16 * k : 16 * k + 16], kv[0, r, k], NT) for k in range(KV)], axis=0
            ) * (HD**-0.5)
            extra = dot(qr, nkv[0, r], NT) * (HD**-0.5)
            extra = jnp.where(fresh_ok, extra, -jnp.inf)
            top = jnp.maximum(
                jnp.max(scores, axis=1, keepdims=True), jnp.max(extra, axis=1, keepdims=True)
            )
            top = jnp.ceil(top * 0.25) * 4.0
            weights = jnp.exp(scores - top)
            extra = jnp.exp(extra - top)
            total = jnp.sum(weights, axis=1, keepdims=True) + jnp.sum(extra, axis=1, keepdims=True)
            low = weights.astype(BF)
            rows_in[r][1].wait()
            mixed = jnp.concatenate(
                [dot(low[16 * k : 16 * k + 16], kv[1, r, k]) for k in range(KV)], axis=0
            ) + dot(extra.astype(BF), nkv[1, r])
            tallies = jnp.where(lane == r, top, jnp.where(lane == 8 + r, total, tallies))
            halves.append(mixed.reshape(16, 8, 128))
        a_send[:, 16 * pair : 16 * pair + 16, :] = jnp.concatenate(halves, axis=1).astype(BF)
    table = jnp.transpose(tallies)[0:16, :].astype(BF)
    a_send[:, 48:64, :] = jnp.broadcast_to(table[None], (16, 16, 128))
    pl.semaphore_wait(barrier, 23)

    def a_copy(i):
        to = plane_peer(i)
        return remote(a_send.at[to], a_recv.at[t], a_ss.at[i], a_rs.at[i], (b, to))

    for i in FAR_PLANE:
        a_copy(i).start()
    a_recv[t] = a_send[t]
    weights_in[1].start()
    weights_in[2].start()

    for copy in inputs[2:]:
        copy.wait()
    choice[...] = jnp.zeros_like(choice)
    for s in range(STEPS):
        choice[4 * s : 4 * s + 4, 0:ROWS] = routes_raw[s].astype(F32) + 1.0
        choice[8 + 4 * s : 12 + 4 * s, 0:ROWS] = rw_raw[s]
    turned = jnp.transpose(choice[...])
    slot_lane = iota((16, 128), 1)
    token_row = iota((16, 128), 0)
    lane_expert = lax.div(slot_lane, 16).astype(F32) + 1.0
    chosen = jnp.zeros((16, 128), F32)
    factor = jnp.zeros((16, 128), F32)
    for k in range(TOP):
        named = jnp.concatenate([turned[0:8, k : k + 1], turned[0:8, 4 + k : 5 + k]], axis=0)
        amount = jnp.concatenate([turned[0:8, 8 + k : 9 + k], turned[0:8, 12 + k : 13 + k]], axis=0)
        hit = named == lane_expert
        chosen = jnp.where(hit, 1.0, chosen)
        factor = jnp.where(hit, amount, factor)
    below = (iota((16, 16), 1) < iota((16, 16), 0)).astype(BF)
    earlier = dot(below, chosen.astype(BF))
    here = (chosen > 0.5) & (earlier.astype(jnp.int32) == lax.rem(slot_lane, 16))
    dispatch = jnp.transpose(
        jnp.concatenate([jnp.where(here, 1.0, 0.0), jnp.zeros((112, 128), F32)], axis=0)
    )[:, 0:16].astype(BF)
    ordered[...] = jnp.zeros_like(ordered)
    combine = jnp.where(here, factor, 0.0)
    for r in range(ROWS):
        for s in range(STEPS):
            ordered[2 * r + s : 2 * r + s + 1, :] = combine[8 * s + r : 8 * s + r + 1]
    combine = ordered[...]
    state[...] = jnp.zeros_like(state)
    combine_high = combine.astype(BF)
    combine_low = (combine - combine_high.astype(F32)).astype(BF)
    mine = pl.ds(pl.multiple_of(t * PART, 128), PART)
    res[...] = jnp.zeros_like(res)
    for r in range(ROWS):
        both = res_raw[r].astype(F32)
        res[r : r + 1, :] = both[0:1]
        res[8 + r : 9 + r, :] = both[1:2]
    res_sum = jnp.sum(res[...], axis=1, keepdims=True)
    res_mine = res[:, mine]
    gain_mine = gain_ref[:, mine]

    def slots(row, slot):
        rank = lax.rem(slot, 16)
        return jnp.where((row == CAP * lax.div(slot, 16) + rank) & (rank < CAP), 1.0, 0.0).astype(BF)

    spans = (16 * NEAR, 16 * (EXPERTS - NEAR))
    packing = [slots(iota((n, w), 0), iota((n, w), 1)) for (_, n), w in zip(GROUPS, spans)]
    unpacking = [slots(iota((w, n), 1), iota((w, n), 0)) for (_, n), w in zip(GROUPS, spans)]
    acc[...] = jnp.zeros_like(acc)
    vacc[...] = jnp.zeros_like(vacc)
    att[...] = jnp.zeros_like(att)
    weights_in[0].wait()

    for i in reversed(FAR_PLANE):
        a_copy(i).wait_recv()

    stats = a_recv[:, 48:64, :].astype(F32)
    tops, totals = stats[:, 0:8], stats[:, 8:16]
    top = jnp.max(tops, axis=0, keepdims=True)
    scale = jnp.exp(tops - top)
    whole = jnp.sum(scale * totals, axis=0, keepdims=True)
    scale = scale / jnp.maximum(whole, 1e-30)
    fcol[...] = jnp.transpose(scale.reshape(128, 128))
    columns = fcol[pl.ds(pl.multiple_of(8 * t, 8), 8), :]
    for pair in range(3):
        both = a_recv[:, 16 * pair : 16 * pair + 16, :].astype(F32)
        for half in range(2):
            r = 2 * pair + half
            joined = jnp.zeros((8, 128), F32)
            for s in range(16):
                joined += both[s, 8 * half : 8 * half + 8] * columns[:, 8 * s + r : 8 * s + r + 1]
            for h in range(3):
                for s in range(STEPS):
                    att[8 * s + r : 8 * s + r + 1, 128 * h : 128 * h + 128] = joined[
                        2 * h + s : 2 * h + s + 1
                    ]

    attended = att[...].astype(BF)
    proj_sum = jnp.zeros((16, 1), F32)
    for s in range(16):
        part = dot(attended, wout[:, PART * s : PART * s + PART])
        proj[s] = part
        proj_sum = proj_sum + jnp.sum(part, axis=1, keepdims=True)
    diagonal = jnp.sum(jnp.where(token_row == slot_lane, proj_sum, 0.0), axis=0, keepdims=True)
    high = diagonal.astype(BF).astype(F32)
    low = diagonal - high
    head = jnp.where(token_row == 6, high, jnp.where(token_row == 7, low, 0.0))
    head = jnp.concatenate([head, jnp.zeros((16, PART - 128), F32)], axis=1)

    def b_copy(i):
        to = plane_peer(i)
        return remote(b_send.at[to], b_recv.at[t], b_ss.at[i], b_rs.at[i], (b, to))

    for i in FAR_PLANE:
        to = plane_peer(i)
        b_send[to] = (proj[to] + head).astype(BF)
        b_copy(i).start()
    b_recv[t] = (proj[t] + head).astype(BF)
    for i in reversed(FAR_PLANE):
        b_copy(i).wait_recv()

    summed = jnp.sum(b_recv[...].astype(F32), axis=0)
    spread = jnp.where(token_row == slot_lane, summed[6:7, 0:128] + summed[7:8, 0:128], 0.0)
    mean = (jnp.sum(spread, axis=1, keepdims=True) + res_sum) * (1.0 / D)
    real = lax.rem(iota((16, PART), 0), 8) < ROWS
    hidden = jnp.where(real, summed + res_mine, 0.0)
    scaled = jnp.where(real, (hidden - mean) * gain_mine, 0.0).astype(BF)

    z_send[...] = dot(dispatch, scaled).astype(BF).reshape(EXPERTS, 16, PART)

    def z_copy(p):
        to = wrap(z + ORDER[p], 8)
        return remote(z_send.at[to], z_recv.at[p], z_ss.at[p], z_rs.at[p], (2 * to + c, t))

    for p in range(7, 0, -1):
        z_copy(p).start()
    z_recv[0] = z_send[z]

    def rows_of(s, group):
        lo, n = GROUPS[group]
        return xall.at[c, s, pl.ds(lo, n)]

    def x1_copy(j, group):
        part = rows_of(t, group)
        n = 2 * j + group
        return remote(part, part, x1_ss.at[n], x1_rs.at[n], (b, place(c, g, wrap(m + j, 4))))

    def x2_copy(j, d, group):
        part = rows_of(place(c, g, wrap(m - j, 4)), group)
        n = 8 * j + 2 * d + group
        return remote(part, part, x2_ss.at[n], x2_rs.at[n], (b, place(c, wrap(g + d, 4), m)))

    def xp_copy(j, d):
        s = place(c, wrap(g - d, 4), wrap(m - j, 4))
        n = 4 * j + d
        return remote(xall.at[c, s], xall.at[c, s], xp_ss.at[n], xp_rs.at[n], (partner, t))

    def multiply(offsets):
        found = [4 * wrap(y - i, 4) + wrap(x - j, 4) for i, j in offsets]
        cols = [pl.ds(pl.multiple_of(s * PART, 128), PART) for s in found]
        both = [jnp.concatenate([xall[c, s], xall[1 - c, s]], axis=0) for s in found]
        rows = jnp.concatenate(both, axis=1)
        for u in range(2):
            units = jnp.concatenate([win[u, :, col] for col in cols], axis=1)
            acc[u] += dot(rows, units, NT)
        squares = vacc[...]
        for part, col in zip(both, cols):
            plain = part.astype(F32) * (1.0 / gain_ref[:, col])
            plain = plain * plain
            squares += plain[:, 0:128] + plain[:, 128:256] + plain[:, 256:384]
        vacc[...] = squares

    for group in range(2):
        span = range(1, NEAR) if group == 0 else range(NEAR, EXPERTS)
        for p in span:
            z_copy(p).wait_recv()
        blocks = z_recv[0:NEAR] if group == 0 else z_recv[NEAR:EXPERTS]
        lo, n = GROUPS[group]
        xall[c, t, lo : lo + n] = dot(
            packing[group], blocks.reshape(spans[group], PART)
        ).astype(BF)
        for j in FAR_RING:
            x1_copy(j, group).start()
        for d in FAR_RING:
            x2_copy(0, d, group).start()
    xp_copy(0, 0).start()
    for r in range(ROWS):
        for s in range(STEPS):
            state[2 * r + s : 2 * r + s + 1, :] = hidden[8 * s + r : 8 * s + r + 1]
    weights_in[1].wait()
    weights_in[2].wait()
    for group in range(2):
        for j in (1, 3, 2):
            x1_copy(j, group).wait_recv()
            for d in FAR_RING:
                x2_copy(j, d, group).start()
            if group:
                xp_copy(j, 0).start()
    for d in FAR_RING:
        for group in range(2):
            x2_copy(0, d, group).wait_recv()
        xp_copy(0, d).start()
    for n in range(4):
        xp_copy(n, 0).wait_recv()
    for d in FAR_RING:
        xp_copy(0, d).wait_recv()
    multiply([(0, 0), (0, 1), (0, 2), (0, 3), (1, 0), (2, 0), (3, 0)])
    for j in (1, 3, 2):
        for d in FAR_RING:
            for group in range(2):
                x2_copy(j, d, group).wait_recv()
            xp_copy(j, d).start()
    for j in (1, 3, 2):
        for d in FAR_RING:
            xp_copy(j, d).wait_recv()
    multiply([(i, j) for i in (1, 2, 3) for j in (1, 2, 3)])

    inverse = lax.rsqrt(jnp.sum(vacc[...], axis=1, keepdims=True) * (1.0 / D) + EPS)
    gate, up = acc[0] * inverse, acc[1] * inverse
    hid[...] = (gate / (1.0 + jnp.exp(-gate)) * up).astype(BF)

    def tiles(lo, found):
        cols = [wdn[:, pl.ds(pl.multiple_of(s * PART, 128), PART)] for s in found]
        slab = dot(hid[lo : lo + PACK], jnp.concatenate(cols, axis=1))
        return [slab[:, PART * i : PART * i + PART] for i in range(4)]

    def q_copy(j):
        part = pl.ds(4 * j, 4)
        return remote(q_send.at[part], q_recv.at[part], q_ss.at[j], q_rs.at[j], (partner, t))

    def g_copy(j, d, group):
        n = 3 * j + d - 1
        k = 2 * n + group
        lo, rows = GROUPS[group]
        part = pl.ds(lo, rows)
        return remote(
            g_send.at[n, part], g_recv.at[n, part], g_ss.at[k], g_rs.at[k],
            (b, place(c, wrap(g + d, 4), m)),
        )

    def m_copy(j, group):
        k = 2 * j + group
        lo, rows = GROUPS[group]
        part = pl.ds(lo, rows)
        return remote(
            m_send.at[j, part], m_recv.at[j, part], m_ss.at[k], m_rs.at[k],
            (b, place(c, g, wrap(m + j, 4))),
        )

    def y_copy(p):
        to = wrap(z - ORDER[p], 8)
        return remote(y_send.at[p], y_recv.at[z], y_ss.at[p], y_rs.at[p], (2 * to + c, t))

    for j in MEMBERS:
        found = [place(1 - c, wrap(m + d, 4), wrap(g + j, 4)) for d in range(4)]
        for d, tile in enumerate(tiles(PACK, found)):
            q_send[4 * j + d] = tile.astype(BF)
        q_copy(j).start()
        found = [place(c, wrap(g + d, 4), wrap(m + j, 4)) for d in range(4)]
        for d, tile in enumerate(tiles(0, found)):
            own[4 * j + d] = tile

    for group in (1, 0):
        lo, n = GROUPS[group]
        for j in MEMBERS:
            if group:
                q_copy(j).wait_recv()
            for d in FAR_RING:
                k = 4 * j + d
                g_send[3 * j + d - 1, lo : lo + n] = (
                    own[k, lo : lo + n] + q_recv[k, lo : lo + n].astype(F32)
                ).astype(BF)
                g_copy(j, d, group).start()

    finals = [None, None]
    for group in (1, 0):
        lo, n = GROUPS[group]
        for j in MEMBERS:
            whole = own[4 * j, lo : lo + n] + q_recv[4 * j, lo : lo + n].astype(F32)
            for d in FAR_RING:
                g_copy(j, d, group).wait_recv()
                whole = whole + g_recv[3 * j + d - 1, lo : lo + n].astype(F32)
            if j:
                m_send[j, lo : lo + n] = whole.astype(BF)
                m_copy(j, group).start()
            else:
                finals[group] = whole

    for group in (1, 0):
        lo, n = GROUPS[group]
        final = finals[group]
        for j in (1, 3, 2):
            m_copy(j, group).wait_recv()
            final = final + m_recv[j, lo : lo + n].astype(F32)
        back = dot(unpacking[group], final.astype(BF)).astype(BF)
        if group:
            y_send[NEAR:EXPERTS] = back.reshape(EXPERTS - NEAR, 16, PART)
            for p in (7, 6, 5):
                y_copy(p).start()
        else:
            y_send[0:NEAR] = back.reshape(NEAR, 16, PART)
            for p in (4, 3, 2, 1):
                y_copy(p).start()
            y_recv[z] = y_send[0]

    for i in FAR_PLANE:
        a_copy(i).wait_send()
        b_copy(i).wait_send()
    for p in range(1, 8):
        z_copy(p).wait_send()
    for j in range(4):
        q_copy(j).wait_send()
        for d in range(4):
            xp_copy(j, d).wait_send()
    for group in range(2):
        for j in FAR_RING:
            x1_copy(j, group).wait_send()
            m_copy(j, group).wait_send()
        for j in range(4):
            for d in FAR_RING:
                x2_copy(j, d, group).wait_send()
                g_copy(j, d, group).wait_send()

    for p in range(1, 8):
        y_copy(p).wait_recv()
    returned = y_recv[...].reshape(128, PART)
    mix = dot(combine_high, returned) + dot(combine_low, returned)
    out_ref[...] = (state[...] + mix).astype(BF)
    for p in range(1, 8):
        y_copy(p).wait_send()


def body(queries, new_kv, cache, residual, w_out, norm_gain, routes, route_weight, w_in, w_down):
    fresh = new_kv.reshape(2, ROWS, STEPS, KV, HD).transpose(0, 1, 3, 2, 4)
    fresh = fresh.reshape(2, ROWS, 16, HD)
    w_in_t = w_in.transpose(0, 2, 3, 1).reshape(2, UNITS, D)
    w_down = w_down.reshape(UNITS, D)
    gain = norm_gain.reshape(1, D)
    chosen = routes.transpose(1, 2, 0)
    factors = route_weight.transpose(1, 2, 0)
    hbm = pl.BlockSpec(memory_space=pltpu.HBM)
    dma = pltpu.SemaphoreType.DMA
    vmem = pltpu.VMEM
    out = pl.pallas_call(
        kernel,
        out_shape=jax.ShapeDtypeStruct((16, PART), BF),
        in_specs=[hbm] * 10,
        out_specs=pl.BlockSpec(memory_space=pltpu.VMEM),
        scratch_shapes=[
            vmem((ROWS, STEPS, D), BF),
            vmem((2, ROWS, 16, HD), BF),
            vmem((ROWS, STEPS, D), BF),
            vmem((1, D), F32),
            vmem((STEPS, TOP, ROWS), jnp.int32),
            vmem((STEPS, TOP, ROWS), F32),
            vmem((ROWS, 128, HD), BF),
            vmem((16, D), F32),
            vmem((128, 128), F32),
            vmem((16, 128), F32),
            vmem((2, ROWS, KV, KEYS, HD), BF),
            vmem((PART, D), BF),
            vmem((2, UNITS, D), BF),
            vmem((UNITS, D), BF),
            vmem((16, 64, 128), BF),
            vmem((16, 64, 128), BF),
            vmem((128, 128), F32),
            vmem((128, 128), F32),
            vmem((16, PART), F32),
            vmem((16, 16, PART), F32),
            vmem((16, 16, PART), BF),
            vmem((16, 16, PART), BF),
            vmem((16, PART), F32),
            vmem((EXPERTS, 16, PART), BF),
            vmem((EXPERTS, 16, PART), BF),
            vmem((2, 16, PACK, PART), BF),
            vmem((2, 2 * PACK, UNITS), F32),
            vmem((2 * PACK, 128), F32),
            vmem((2 * PACK, UNITS), BF),
            vmem((16, PACK, PART), F32),
            vmem((16, PACK, PART), BF),
            vmem((16, PACK, PART), BF),
            vmem((12, PACK, PART), BF),
            vmem((12, PACK, PART), BF),
            vmem((4, PACK, PART), BF),
            vmem((4, PACK, PART), BF),
            vmem((EXPERTS, 16, PART), BF),
            vmem((EXPERTS, 16, PART), BF),
            dma((6,)),
            dma((2, ROWS)),
            dma((3,)),
            dma((16,)), dma((16,)),
            dma((16,)), dma((16,)),
            dma((8,)), dma((8,)),
            dma((8,)), dma((8,)),
            dma((32,)), dma((32,)),
            dma((16,)), dma((16,)),
            dma((4,)), dma((4,)),
            dma((24,)), dma((24,)),
            dma((8,)), dma((8,)),
            dma((8,)), dma((8,)),
        ],
        compiler_params=pltpu.CompilerParams(
            collective_id=0, has_side_effects=True, vmem_limit_bytes=56 * 1024 * 1024
        ),
        name="layer",
    )(queries, fresh, cache, residual, w_out, gain, chosen, factors, w_in_t, w_down)
    return out[:12].reshape(ROWS, STEPS, PART)


def solution(mesh):
    return jax.shard_map(
        body,
        mesh=mesh,
        in_specs=(
            P("expert", None, None),
            P(None, "expert", None, None),
            P(None, "expert", None, "tensor", None),
            P("expert", None, None),
            P("tensor", None),
            P(),
            P("expert", None, None),
            P("expert", None, None),
            P("expert", None, None, "tensor"),
            P("expert", "tensor", None),
        ),
        out_specs=P("expert", None, "tensor"),
        check_vma=False,
    )
```

```python
import jax
import jax.numpy as jnp
from jax import lax
from jax.experimental import pallas as pl
from jax.experimental.pallas import tpu as pltpu
from jax.sharding import PartitionSpec as P

D = 6144
HEADS = 48
KV = 8
HD = 128
EXPERTS = 8
TOP = 4
CAP = 9
ROWS = 6
STEPS = 2
KEYS = 256
UNITS = 168
PART = 384
PACK = 80
EPS = 1e-05
BF = jnp.bfloat16
F32 = jnp.float32
MESH = pl.DeviceIdType.MESH
NT = (((1,), (1,)), ((), ()))
FAR_Z = (4, 3, 5, 2, 6, 1, 7)
FAR_PLANE = (10, 6, 9, 11, 14, 2, 8, 5, 7, 13, 15, 1, 3, 4, 12)
FAR_RING = (2, 1, 3)
ORDER = (0, 1, 7, 2, 6, 3, 5, 4)
NEAR = 5
GROUPS = ((0, 48), (48, 32))
MEMBERS = (2, 1, 3, 0)


def wrap(value, size):
    return lax.rem(value + size, size)


def iota(shape, dim):
    return lax.broadcasted_iota(jnp.int32, shape, dim)


def dot(a, b, dims=None):
    if dims is None:
        return jnp.dot(a, b, preferred_element_type=F32)
    return lax.dot_general(a, b, dims, preferred_element_type=F32)


def kernel(
    q_hbm, nkv_hbm, cache_hbm, res_hbm, wout_hbm, gain_hbm, routes_hbm, rw_hbm, win_hbm, wdn_hbm,
    out_ref,
    q_raw, nkv, res_raw, gain_ref, routes_raw, rw_raw, q_ref, res, choice, ordered,
    kv, wout, win, wdn,
    a_send, a_recv, stat, fcol, att, proj, b_send, b_recv,
    state, z_send, z_recv, xall, acc, vacc, hid,
    own, q_send, q_recv, g_send, g_recv, m_send, m_recv, y_send, y_recv,
    in_sem, kv_sem, w_sem, sent, one_rs, z_rs, x1_rs, x2_rs, xp_rs, q_rs, g_rs, m_rs,
):
    b = lax.axis_index("expert")
    t = lax.axis_index("tensor")
    z, c = lax.div(b, 2), lax.rem(b, 2)
    y, x = lax.div(t, 4), lax.rem(t, 4)
    partner = 2 * z + 1 - c
    m = (1 - c) * x + c * y
    g = (1 - c) * y + c * x

    def place(core, group, member):
        return (1 - core) * (4 * group + member) + core * (4 * member + group)

    def plane_peer(i):
        return 4 * wrap(y + i // 4, 4) + wrap(x + i % 4, 4)

    def remote(src, dst, ss, rs, dev):
        return pltpu.make_async_remote_copy(
            src_ref=src, dst_ref=dst, send_sem=ss, recv_sem=rs, device_id=dev, device_id_type=MESH
        )

    def settle(ref, sem):
        pltpu.make_async_copy(ref, ref, sem).wait()

    inputs = [
        pltpu.make_async_copy(src, dst, in_sem.at[i])
        for i, (src, dst) in enumerate(
            [
                (q_hbm, q_raw), (nkv_hbm, nkv), (res_hbm, res_raw), (gain_hbm, gain_ref),
                (routes_hbm, routes_raw), (rw_hbm, rw_raw),
            ]
        )
    ]
    rows_in = [
        [
            pltpu.make_async_copy(cache_hbm.at[s, r], kv.at[s, r], kv_sem.at[s, r])
            for s in range(2)
        ]
        for r in range(ROWS)
    ]
    weights_in = [
        pltpu.make_async_copy(wout_hbm, wout, w_sem.at[0]),
        pltpu.make_async_copy(win_hbm, win, w_sem.at[1]),
        pltpu.make_async_copy(wdn_hbm, wdn, w_sem.at[2]),
    ]
    inputs[0].start()
    inputs[1].start()
    for pair in rows_in[:3]:
        for copy in pair:
            copy.start()

    barrier = pltpu.get_barrier_semaphore()

    def greet(dev):
        pl.semaphore_signal(barrier, inc=1, device_id=dev, device_id_type=MESH)

    for d in FAR_Z:
        greet((2 * wrap(z + d, 8) + c, t))
    for i in FAR_PLANE:
        greet((b, plane_peer(i)))
    greet((partner, t))

    inputs[0].wait()
    nothing = jnp.zeros((2, HD), F32)
    for r in range(ROWS):
        both = q_raw[r].astype(F32)
        pieces = []
        for owner in range(16):
            for h in range(3):
                lo = HD * (3 * owner + h)
                pieces.append(both[:, lo : lo + HD])
            pieces.append(nothing)
        q_ref[r] = jnp.concatenate(pieces, axis=0).astype(BF)
    inputs[1].wait()

    row_id = iota((128, 16), 0)
    key_id = iota((128, 16), 1)
    fresh_ok = (
        (lax.div(row_id, 16) == lax.div(key_id, 2))
        & (lax.rem(key_id, 2) <= lax.rem(row_id, 2))
        & (jnp.broadcast_to(t, (128, 16)) == 0)
    )
    lane = iota((128, 128), 1)
    tallies = jnp.zeros((128, 128), F32)
    for pair in range(3):
        halves = []
        for r in (2 * pair, 2 * pair + 1):
            rows_in[r][0].wait()
            if r + 3 < ROWS:
                for copy in rows_in[r + 3]:
                    copy.start()
            if r == 3:
                for copy in inputs[2:] + weights_in[:1]:
                    copy.start()
            qr = q_ref[r]
            scores = jnp.concatenate(
                [dot(qr[16 * k : 16 * k + 16], kv[0, r, k], NT) for k in range(KV)], axis=0
            ) * (HD**-0.5)
            extra = dot(qr, nkv[0, r], NT) * (HD**-0.5)
            extra = jnp.where(fresh_ok, extra, -jnp.inf)
            top = jnp.maximum(
                jnp.max(scores, axis=1, keepdims=True), jnp.max(extra, axis=1, keepdims=True)
            )
            top = jnp.ceil(top * 0.25) * 4.0
            weights = jnp.exp(scores - top)
            extra = jnp.exp(extra - top)
            total = jnp.sum(weights, axis=1, keepdims=True) + jnp.sum(extra, axis=1, keepdims=True)
            low = weights.astype(BF)
            rows_in[r][1].wait()
            mixed = jnp.concatenate(
                [dot(low[16 * k : 16 * k + 16], kv[1, r, k]) for k in range(KV)], axis=0
            ) + dot(extra.astype(BF), nkv[1, r])
            tallies = jnp.where(lane == r, top, jnp.where(lane == 8 + r, total, tallies))
            halves.append(mixed.reshape(16, 8, 128))
        a_send[:, 16 * pair : 16 * pair + 16, :] = jnp.concatenate(halves, axis=1).astype(BF)
    table = jnp.transpose(tallies)[0:16, :].astype(BF)
    a_send[:, 48:64, :] = jnp.broadcast_to(table[None], (16, 16, 128))
    pl.semaphore_wait(barrier, 23)

    def a_copy(i):
        to = plane_peer(i)
        return remote(a_send.at[to], a_recv.at[t], sent.at[0], one_rs.at[0], (b, to))

    for i in FAR_PLANE:
        a_copy(i).start()
    a_recv[t] = a_send[t]
    weights_in[1].start()
    weights_in[2].start()

    for copy in inputs[2:]:
        copy.wait()
    choice[...] = jnp.zeros_like(choice)
    for s in range(STEPS):
        choice[4 * s : 4 * s + 4, 0:ROWS] = routes_raw[s].astype(F32) + 1.0
        choice[8 + 4 * s : 12 + 4 * s, 0:ROWS] = rw_raw[s]
    turned = jnp.transpose(choice[...])
    slot_lane = iota((16, 128), 1)
    token_row = iota((16, 128), 0)
    lane_expert = lax.div(slot_lane, 16).astype(F32) + 1.0
    chosen = jnp.zeros((16, 128), F32)
    factor = jnp.zeros((16, 128), F32)
    for k in range(TOP):
        named = jnp.concatenate([turned[0:8, k : k + 1], turned[0:8, 4 + k : 5 + k]], axis=0)
        amount = jnp.concatenate([turned[0:8, 8 + k : 9 + k], turned[0:8, 12 + k : 13 + k]], axis=0)
        hit = named == lane_expert
        chosen = jnp.where(hit, 1.0, chosen)
        factor = jnp.where(hit, amount, factor)
    below = (iota((16, 16), 1) < iota((16, 16), 0)).astype(BF)
    earlier = dot(below, chosen.astype(BF))
    here = (chosen > 0.5) & (earlier.astype(jnp.int32) == lax.rem(slot_lane, 16))
    dispatch = jnp.transpose(
        jnp.concatenate([jnp.where(here, 1.0, 0.0), jnp.zeros((112, 128), F32)], axis=0)
    )[:, 0:16].astype(BF)
    ordered[...] = jnp.zeros_like(ordered)
    combine = jnp.where(here, factor, 0.0)
    for r in range(ROWS):
        for s in range(STEPS):
            ordered[2 * r + s : 2 * r + s + 1, :] = combine[8 * s + r : 8 * s + r + 1]
    combine = ordered[...]
    state[...] = jnp.zeros_like(state)
    combine_high = combine.astype(BF)
    combine_low = (combine - combine_high.astype(F32)).astype(BF)
    mine = pl.ds(pl.multiple_of(t * PART, 128), PART)
    res[...] = jnp.zeros_like(res)
    for r in range(ROWS):
        both = res_raw[r].astype(F32)
        res[r : r + 1, :] = both[0:1]
        res[8 + r : 9 + r, :] = both[1:2]
    res_sum = jnp.sum(res[...], axis=1, keepdims=True)
    res_mine = res[:, mine]
    gain_mine = gain_ref[:, mine]

    def slots(row, slot):
        rank = lax.rem(slot, 16)
        return jnp.where((row == CAP * lax.div(slot, 16) + rank) & (rank < CAP), 1.0, 0.0).astype(BF)

    spans = (16 * NEAR, 16 * (EXPERTS - NEAR))
    packing = [slots(iota((n, w), 0), iota((n, w), 1)) for (_, n), w in zip(GROUPS, spans)]
    unpacking = [slots(iota((w, n), 1), iota((w, n), 0)) for (_, n), w in zip(GROUPS, spans)]
    acc[...] = jnp.zeros_like(acc)
    vacc[...] = jnp.zeros_like(vacc)
    att[...] = jnp.zeros_like(att)
    weights_in[0].wait()

    settle(a_recv.at[pl.ds(0, 15)], one_rs.at[0])

    stats = a_recv[:, 48:64, :].astype(F32)
    tops, totals = stats[:, 0:8], stats[:, 8:16]
    top = jnp.max(tops, axis=0, keepdims=True)
    scale = jnp.exp(tops - top)
    whole = jnp.sum(scale * totals, axis=0, keepdims=True)
    scale = scale / jnp.maximum(whole, 1e-30)
    fcol[...] = jnp.transpose(scale.reshape(128, 128))
    columns = fcol[pl.ds(pl.multiple_of(8 * t, 8), 8), :]
    for pair in range(3):
        both = a_recv[:, 16 * pair : 16 * pair + 16, :].astype(F32)
        for half in range(2):
            r = 2 * pair + half
            joined = jnp.zeros((8, 128), F32)
            for s in range(16):
                joined += both[s, 8 * half : 8 * half + 8] * columns[:, 8 * s + r : 8 * s + r + 1]
            for h in range(3):
                for s in range(STEPS):
                    att[8 * s + r : 8 * s + r + 1, 128 * h : 128 * h + 128] = joined[
                        2 * h + s : 2 * h + s + 1
                    ]

    attended = att[...].astype(BF)
    proj_sum = jnp.zeros((16, 1), F32)
    for s in range(16):
        part = dot(attended, wout[:, PART * s : PART * s + PART])
        proj[s] = part
        proj_sum = proj_sum + jnp.sum(part, axis=1, keepdims=True)
    diagonal = jnp.sum(jnp.where(token_row == slot_lane, proj_sum, 0.0), axis=0, keepdims=True)
    high = diagonal.astype(BF).astype(F32)
    low = diagonal - high
    head = jnp.where(token_row == 6, high, jnp.where(token_row == 7, low, 0.0))
    head = jnp.concatenate([head, jnp.zeros((16, PART - 128), F32)], axis=1)

    def b_copy(i):
        to = plane_peer(i)
        return remote(b_send.at[to], b_recv.at[t], sent.at[1], one_rs.at[1], (b, to))

    for i in FAR_PLANE:
        to = plane_peer(i)
        b_send[to] = (proj[to] + head).astype(BF)
        b_copy(i).start()
    b_recv[t] = (proj[t] + head).astype(BF)
    settle(b_recv.at[pl.ds(0, 15)], one_rs.at[1])

    summed = jnp.sum(b_recv[...].astype(F32), axis=0)
    spread = jnp.where(token_row == slot_lane, summed[6:7, 0:128] + summed[7:8, 0:128], 0.0)
    mean = (jnp.sum(spread, axis=1, keepdims=True) + res_sum) * (1.0 / D)
    real = lax.rem(iota((16, PART), 0), 8) < ROWS
    hidden = jnp.where(real, summed + res_mine, 0.0)
    scaled = jnp.where(real, (hidden - mean) * gain_mine, 0.0).astype(BF)

    z_send[...] = dot(dispatch, scaled).astype(BF).reshape(EXPERTS, 16, PART)

    def z_copy(p):
        to = wrap(z + ORDER[p], 8)
        return remote(z_send.at[to], z_recv.at[p], sent.at[2], z_rs.at[int(p >= NEAR)], (2 * to + c, t))

    for p in range(7, 0, -1):
        z_copy(p).start()
    z_recv[0] = z_send[z]

    def rows_of(s, group):
        lo, n = GROUPS[group]
        return xall.at[c, s, pl.ds(lo, n)]

    def x1_copy(j, group):
        part = rows_of(t, group)
        n = 2 * (j - 1) + group
        return remote(part, part, sent.at[3], x1_rs.at[n], (b, place(c, g, wrap(m + j, 4))))

    def x2_copy(j, d, group):
        part = rows_of(place(c, g, wrap(m - j, 4)), group)
        return remote(part, part, sent.at[4], x2_rs.at[j], (b, place(c, wrap(g + d, 4), m)))

    def xp_copy(j, d):
        s = place(c, wrap(g - d, 4), wrap(m - j, 4))
        late = int(j > 0 and d > 0)
        return remote(xall.at[c, s], xall.at[c, s], sent.at[5], xp_rs.at[late], (partner, t))

    def multiply(offsets):
        found = [4 * wrap(y - i, 4) + wrap(x - j, 4) for i, j in offsets]
        cols = [pl.ds(pl.multiple_of(s * PART, 128), PART) for s in found]
        both = [jnp.concatenate([xall[c, s], xall[1 - c, s]], axis=0) for s in found]
        rows = jnp.concatenate(both, axis=1)
        for u in range(2):
            units = jnp.concatenate([win[u, :, col] for col in cols], axis=1)
            acc[u] += dot(rows, units, NT)
        squares = vacc[...]
        for part, col in zip(both, cols):
            plain = part.astype(F32) * (1.0 / gain_ref[:, col])
            plain = plain * plain
            squares += plain[:, 0:128] + plain[:, 128:256] + plain[:, 256:384]
        vacc[...] = squares

    for group in range(2):
        came = pl.ds(NEAR, EXPERTS - NEAR) if group else pl.ds(1, NEAR - 1)
        settle(z_recv.at[came], z_rs.at[group])
        blocks = z_recv[0:NEAR] if group == 0 else z_recv[NEAR:EXPERTS]
        lo, n = GROUPS[group]
        xall[c, t, lo : lo + n] = dot(
            packing[group], blocks.reshape(spans[group], PART)
        ).astype(BF)
        for j in FAR_RING:
            x1_copy(j, group).start()
        for d in FAR_RING:
            x2_copy(0, d, group).start()
    xp_copy(0, 0).start()
    for r in range(ROWS):
        for s in range(STEPS):
            state[2 * r + s : 2 * r + s + 1, :] = hidden[8 * s + r : 8 * s + r + 1]
    weights_in[1].wait()
    weights_in[2].wait()
    for group in range(2):
        for j in (1, 3, 2):
            x1_copy(j, group).wait_recv()
            for d in FAR_RING:
                x2_copy(j, d, group).start()
            if group:
                xp_copy(j, 0).start()
    settle(xall.at[0, pl.ds(0, 3)], x2_rs.at[0])
    for d in FAR_RING:
        xp_copy(0, d).start()
    settle(xall.at[0, pl.ds(0, 7)], xp_rs.at[0])
    multiply([(0, 0), (0, 1), (0, 2), (0, 3), (1, 0), (2, 0), (3, 0)])
    for j in (1, 3, 2):
        settle(xall.at[0, pl.ds(0, 3)], x2_rs.at[j])
        for d in FAR_RING:
            xp_copy(j, d).start()
    settle(xall.at[0, pl.ds(0, 9)], xp_rs.at[1])
    multiply([(i, j) for i in (1, 2, 3) for j in (1, 2, 3)])

    inverse = lax.rsqrt(jnp.sum(vacc[...], axis=1, keepdims=True) * (1.0 / D) + EPS)
    gate, up = acc[0] * inverse, acc[1] * inverse
    hid[...] = (gate / (1.0 + jnp.exp(-gate)) * up).astype(BF)

    def tiles(lo, found):
        cols = [wdn[:, pl.ds(pl.multiple_of(s * PART, 128), PART)] for s in found]
        slab = dot(hid[lo : lo + PACK], jnp.concatenate(cols, axis=1))
        return [slab[:, PART * i : PART * i + PART] for i in range(4)]

    def q_copy(j):
        part = pl.ds(4 * j, 4)
        return remote(q_send.at[part], q_recv.at[part], sent.at[6], q_rs.at[j], (partner, t))

    def g_copy(j, d, group):
        n = 3 * j + d - 1
        lo, rows = GROUPS[group]
        part = pl.ds(lo, rows)
        return remote(
            g_send.at[n, part], g_recv.at[n, part], sent.at[7], g_rs.at[2 * j + group],
            (b, place(c, wrap(g + d, 4), m)),
        )

    def m_copy(j, group):
        lo, rows = GROUPS[group]
        part = pl.ds(lo, rows)
        return remote(
            m_send.at[j, part], m_recv.at[j, part], sent.at[8], m_rs.at[group],
            (b, place(c, g, wrap(m + j, 4))),
        )

    def y_copy(p):
        to = wrap(z - ORDER[p], 8)
        return remote(y_send.at[p], y_recv.at[z], sent.at[9], one_rs.at[2], (2 * to + c, t))

    for j in MEMBERS:
        found = [place(1 - c, wrap(m + d, 4), wrap(g + j, 4)) for d in range(4)]
        for d, tile in enumerate(tiles(PACK, found)):
            q_send[4 * j + d] = tile.astype(BF)
        q_copy(j).start()
        found = [place(c, wrap(g + d, 4), wrap(m + j, 4)) for d in range(4)]
        for d, tile in enumerate(tiles(0, found)):
            own[4 * j + d] = tile

    for group in (1, 0):
        lo, n = GROUPS[group]
        for j in MEMBERS:
            if group:
                q_copy(j).wait_recv()
            for d in FAR_RING:
                k = 4 * j + d
                g_send[3 * j + d - 1, lo : lo + n] = (
                    own[k, lo : lo + n] + q_recv[k, lo : lo + n].astype(F32)
                ).astype(BF)
                g_copy(j, d, group).start()

    finals = [None, None]
    for group in (1, 0):
        lo, n = GROUPS[group]
        for j in MEMBERS:
            whole = own[4 * j, lo : lo + n] + q_recv[4 * j, lo : lo + n].astype(F32)
            settle(g_recv.at[pl.ds(0, 3), pl.ds(lo, n)], g_rs.at[2 * j + group])
            for d in FAR_RING:
                whole = whole + g_recv[3 * j + d - 1, lo : lo + n].astype(F32)
            if j:
                m_send[j, lo : lo + n] = whole.astype(BF)
                m_copy(j, group).start()
            else:
                finals[group] = whole

    for group in (1, 0):
        lo, n = GROUPS[group]
        final = finals[group]
        settle(m_recv.at[pl.ds(0, 3), pl.ds(lo, n)], m_rs.at[group])
        for j in (1, 3, 2):
            final = final + m_recv[j, lo : lo + n].astype(F32)
        back = dot(unpacking[group], final.astype(BF)).astype(BF)
        if group:
            y_send[NEAR:EXPERTS] = back.reshape(EXPERTS - NEAR, 16, PART)
            for p in (7, 6, 5):
                y_copy(p).start()
        else:
            y_send[0:NEAR] = back.reshape(NEAR, 16, PART)
            for p in (4, 3, 2, 1):
                y_copy(p).start()
            y_recv[z] = y_send[0]

    settle(a_send.at[pl.ds(0, 15)], sent.at[0])
    settle(b_send.at[pl.ds(0, 15)], sent.at[1])
    settle(z_send.at[pl.ds(0, 7)], sent.at[2])
    settle(xall.at[0, pl.ds(0, 3)], sent.at[3])
    settle(xall.at[0, pl.ds(0, 12)], sent.at[4])
    settle(xall.at[0], sent.at[5])
    settle(q_send, sent.at[6])
    settle(g_send, sent.at[7])
    settle(m_send.at[pl.ds(0, 3)], sent.at[8])

    settle(y_recv.at[pl.ds(0, 7)], one_rs.at[2])
    returned = y_recv[...].reshape(128, PART)
    mix = dot(combine_high, returned) + dot(combine_low, returned)
    out_ref[...] = (state[...] + mix).astype(BF)
    settle(y_send.at[pl.ds(0, 7)], sent.at[9])


def body(queries, new_kv, cache, residual, w_out, norm_gain, routes, route_weight, w_in, w_down):
    fresh = new_kv.reshape(2, ROWS, STEPS, KV, HD).transpose(0, 1, 3, 2, 4)
    fresh = fresh.reshape(2, ROWS, 16, HD)
    w_in_t = w_in.transpose(0, 2, 3, 1).reshape(2, UNITS, D)
    w_down = w_down.reshape(UNITS, D)
    gain = norm_gain.reshape(1, D)
    chosen = routes.transpose(1, 2, 0)
    factors = route_weight.transpose(1, 2, 0)
    hbm = pl.BlockSpec(memory_space=pltpu.HBM)
    dma = pltpu.SemaphoreType.DMA
    vmem = pltpu.VMEM
    out = pl.pallas_call(
        kernel,
        out_shape=jax.ShapeDtypeStruct((16, PART), BF),
        in_specs=[hbm] * 10,
        out_specs=pl.BlockSpec(memory_space=pltpu.VMEM),
        scratch_shapes=[
            vmem((ROWS, STEPS, D), BF),
            vmem((2, ROWS, 16, HD), BF),
            vmem((ROWS, STEPS, D), BF),
            vmem((1, D), F32),
            vmem((STEPS, TOP, ROWS), jnp.int32),
            vmem((STEPS, TOP, ROWS), F32),
            vmem((ROWS, 128, HD), BF),
            vmem((16, D), F32),
            vmem((128, 128), F32),
            vmem((16, 128), F32),
            vmem((2, ROWS, KV, KEYS, HD), BF),
            vmem((PART, D), BF),
            vmem((2, UNITS, D), BF),
            vmem((UNITS, D), BF),
            vmem((16, 64, 128), BF),
            vmem((16, 64, 128), BF),
            vmem((128, 128), F32),
            vmem((128, 128), F32),
            vmem((16, PART), F32),
            vmem((16, 16, PART), F32),
            vmem((16, 16, PART), BF),
            vmem((16, 16, PART), BF),
            vmem((16, PART), F32),
            vmem((EXPERTS, 16, PART), BF),
            vmem((EXPERTS, 16, PART), BF),
            vmem((2, 16, PACK, PART), BF),
            vmem((2, 2 * PACK, UNITS), F32),
            vmem((2 * PACK, 128), F32),
            vmem((2 * PACK, UNITS), BF),
            vmem((16, PACK, PART), F32),
            vmem((16, PACK, PART), BF),
            vmem((16, PACK, PART), BF),
            vmem((12, PACK, PART), BF),
            vmem((12, PACK, PART), BF),
            vmem((4, PACK, PART), BF),
            vmem((4, PACK, PART), BF),
            vmem((EXPERTS, 16, PART), BF),
            vmem((EXPERTS, 16, PART), BF),
            dma((6,)), dma((2, ROWS)), dma((3,)), dma((10,)), dma((3,)),
            dma((2,)), dma((6,)), dma((4,)), dma((2,)), dma((4,)), dma((8,)), dma((2,)),
        ],
        compiler_params=pltpu.CompilerParams(
            collective_id=0, has_side_effects=True, vmem_limit_bytes=56 * 1024 * 1024
        ),
        name="layer",
    )(queries, fresh, cache, residual, w_out, gain, chosen, factors, w_in_t, w_down)
    return out[:12].reshape(ROWS, STEPS, PART)


def solution(mesh):
    return jax.shard_map(
        body,
        mesh=mesh,
        in_specs=(
            P("expert", None, None),
            P(None, "expert", None, None),
            P(None, "expert", None, "tensor", None),
            P("expert", None, None),
            P("tensor", None),
            P(),
            P("expert", None, None),
            P("expert", None, None),
            P("expert", None, None, "tensor"),
            P("expert", "tensor", None),
        ),
        out_specs=P("expert", None, "tensor"),
        check_vma=False,
    )
```

```python
import jax
import jax.numpy as jnp
from jax import lax
from jax.experimental import pallas as pl
from jax.experimental.pallas import tpu as pltpu
from jax.sharding import PartitionSpec as P

D = 6144
HEADS = 48
KV = 8
HD = 128
EXPERTS = 8
TOP = 4
CAP = 9
ROWS = 6
STEPS = 2
KEYS = 256
UNITS = 168
PART = 384
PACK = 80
EPS = 1e-05
BF = jnp.bfloat16
F32 = jnp.float32
MESH = pl.DeviceIdType.MESH
NT = (((1,), (1,)), ((), ()))
FAR_Z = (4, 3, 5, 2, 6, 1, 7)
FAR_PLANE = (10, 6, 9, 11, 14, 2, 8, 5, 7, 13, 15, 1, 3, 4, 12)
FAR_RING = (2, 1, 3)
ORDER = (0, 1, 7, 2, 6, 3, 5, 4)
NEAR = 3
GROUPS = ((0, 32), (32, 48))
MEMBERS = (1, 3, 2, 0)


def wrap(value, size):
    return lax.rem(value + size, size)


def iota(shape, dim):
    return lax.broadcasted_iota(jnp.int32, shape, dim)


def dot(a, b, dims=None):
    if dims is None:
        return jnp.dot(a, b, preferred_element_type=F32)
    return lax.dot_general(a, b, dims, preferred_element_type=F32)


def kernel(
    q_hbm, nkv_hbm, cache_hbm, res_hbm, wout_hbm, gain_hbm, routes_hbm, rw_hbm, win_hbm, wdn_hbm,
    out_ref,
    q_raw, nkv, res_raw, gain_ref, routes_raw, rw_raw, q_ref, res, choice, ordered,
    kv, wout, win, wdn,
    a_send, a_recv, stat, fcol, att, proj, b_send, b_recv,
    state, z_send, z_recv, xall, acc, vacc, hid,
    own, q_send, q_recv, g_send, g_recv, m_send, m_recv, y_send, y_recv,
    in_sem, kv_sem, w_sem, sent, one_rs, z_rs, x1_rs, x2_rs, xp_rs, q_rs, g_rs, m_rs,
):
    b = lax.axis_index("expert")
    t = lax.axis_index("tensor")
    z, c = lax.div(b, 2), lax.rem(b, 2)
    y, x = lax.div(t, 4), lax.rem(t, 4)
    partner = 2 * z + 1 - c
    m = (1 - c) * x + c * y
    g = (1 - c) * y + c * x

    def place(core, group, member):
        return (1 - core) * (4 * group + member) + core * (4 * member + group)

    def plane_peer(i):
        return 4 * wrap(y + i // 4, 4) + wrap(x + i % 4, 4)

    def remote(src, dst, ss, rs, dev):
        return pltpu.make_async_remote_copy(
            src_ref=src, dst_ref=dst, send_sem=ss, recv_sem=rs, device_id=dev, device_id_type=MESH
        )

    def settle(ref, sem):
        pltpu.make_async_copy(ref, ref, sem).wait()

    inputs = [
        pltpu.make_async_copy(src, dst, in_sem.at[i])
        for i, (src, dst) in enumerate(
            [
                (q_hbm, q_raw), (nkv_hbm, nkv.at[:, :, pl.ds(0, 16)]), (res_hbm, res_raw), (gain_hbm, gain_ref),
                (routes_hbm, routes_raw), (rw_hbm, rw_raw),
            ]
        )
    ]
    rows_in = [
        [
            pltpu.make_async_copy(cache_hbm.at[s, r], kv.at[s, r], kv_sem.at[s, r])
            for s in range(2)
        ]
        for r in range(ROWS)
    ]
    weights_in = [
        pltpu.make_async_copy(wout_hbm, wout, w_sem.at[0]),
        pltpu.make_async_copy(win_hbm, win, w_sem.at[1]),
        pltpu.make_async_copy(wdn_hbm, wdn, w_sem.at[2]),
    ]
    inputs[0].start()
    for pair in rows_in[:3]:
        for copy in pair:
            copy.start()
    nkv[...] = jnp.zeros_like(nkv)
    inputs[1].start()

    barrier = pltpu.get_barrier_semaphore()

    def greet(dev):
        pl.semaphore_signal(barrier, inc=1, device_id=dev, device_id_type=MESH)

    for d in FAR_Z:
        greet((2 * wrap(z + d, 8) + c, t))
    for i in FAR_PLANE:
        greet((b, plane_peer(i)))
    greet((partner, t))

    inputs[0].wait()
    nothing = jnp.zeros((2, HD), F32)
    for r in range(ROWS):
        both = q_raw[r].astype(F32)
        pieces = []
        for owner in range(16):
            for h in range(3):
                lo = HD * (3 * owner + h)
                pieces.append(both[:, lo : lo + HD])
            pieces.append(nothing)
        q_ref[r] = jnp.concatenate(pieces, axis=0).astype(BF)
    inputs[1].wait()

    def a_copy(i, half):
        to = plane_peer(i)
        part = pl.ds(32 * half, 32)
        return remote(
            a_send.at[to, part], a_recv.at[t, part], sent.at[0], one_rs.at[0], (b, to)
        )

    row_id = iota((128, 128), 0)
    key_id = iota((128, 128), 1)
    fresh_ok = (
        (lax.div(row_id, 16) == lax.div(key_id, 2))
        & (lax.rem(key_id, 2) <= lax.rem(row_id, 2))
        & (jnp.broadcast_to(t, (128, 128)) == 0)
    )
    lane = iota((128, 128), 1)
    tallies = jnp.zeros((128, 128), F32)
    for pair in range(3):
        halves = []
        for r in (2 * pair, 2 * pair + 1):
            rows_in[r][0].wait()
            if r + 3 < ROWS:
                for copy in rows_in[r + 3]:
                    copy.start()
            if r == 3:
                for copy in inputs[2:] + weights_in[:1]:
                    copy.start()
            qr = q_ref[r]
            scores = jnp.concatenate(
                [dot(qr[16 * k : 16 * k + 16], kv[0, r, k], NT) for k in range(KV)], axis=0
            ) * (HD**-0.5)
            extra = dot(qr, nkv[0, r], NT) * (HD**-0.5)
            extra = jnp.where(fresh_ok, extra, -jnp.inf)
            top = jnp.maximum(jnp.maximum(scores[:, 0:128], scores[:, 128:256]), extra)
            top = jnp.ceil(jnp.max(top, axis=1, keepdims=True) * 0.25) * 4.0
            weights = jnp.exp(scores - top)
            extra = jnp.exp(extra - top)
            total = weights[:, 0:128] + weights[:, 128:256] + extra
            total = jnp.sum(total, axis=1, keepdims=True)
            low = weights.astype(BF)
            rows_in[r][1].wait()
            mixed = jnp.concatenate(
                [dot(low[16 * k : 16 * k + 16], kv[1, r, k]) for k in range(KV)], axis=0
            ) + dot(extra.astype(BF), nkv[1, r])
            tallies = jnp.where(lane == r, top, jnp.where(lane == 8 + r, total, tallies))
            halves.append(mixed.reshape(16, 8, 128))
        a_send[:, 16 * pair : 16 * pair + 16, :] = jnp.concatenate(halves, axis=1).astype(BF)
        if pair == 1:
            pl.semaphore_wait(barrier, 23)
            for i in FAR_PLANE:
                a_copy(i, 0).start()
    table = jnp.transpose(tallies)[0:16, :].astype(BF)
    a_send[:, 48:64, :] = jnp.broadcast_to(table[None], (16, 16, 128))
    for i in FAR_PLANE:
        a_copy(i, 1).start()
    a_recv[t] = a_send[t]
    weights_in[1].start()
    weights_in[2].start()

    for copy in inputs[2:]:
        copy.wait()
    choice[...] = jnp.zeros_like(choice)
    for s in range(STEPS):
        choice[4 * s : 4 * s + 4, 0:ROWS] = routes_raw[s].astype(F32) + 1.0
        choice[8 + 4 * s : 12 + 4 * s, 0:ROWS] = rw_raw[s]
    turned = jnp.transpose(choice[...])
    slot_lane = iota((16, 128), 1)
    token_row = iota((16, 128), 0)
    lane_expert = lax.div(slot_lane, 16).astype(F32) + 1.0
    chosen = jnp.zeros((16, 128), F32)
    factor = jnp.zeros((16, 128), F32)
    for k in range(TOP):
        named = jnp.concatenate([turned[0:8, k : k + 1], turned[0:8, 4 + k : 5 + k]], axis=0)
        amount = jnp.concatenate([turned[0:8, 8 + k : 9 + k], turned[0:8, 12 + k : 13 + k]], axis=0)
        hit = named == lane_expert
        chosen = jnp.where(hit, 1.0, chosen)
        factor = jnp.where(hit, amount, factor)
    below = (iota((16, 16), 1) < iota((16, 16), 0)).astype(BF)
    earlier = dot(below, chosen.astype(BF))
    here = (chosen > 0.5) & (earlier.astype(jnp.int32) == lax.rem(slot_lane, 16))
    dispatch = jnp.transpose(
        jnp.concatenate([jnp.where(here, 1.0, 0.0), jnp.zeros((112, 128), F32)], axis=0)
    )[:, 0:16].astype(BF)
    ordered[...] = jnp.zeros_like(ordered)
    combine = jnp.where(here, factor, 0.0)
    for r in range(ROWS):
        for s in range(STEPS):
            ordered[2 * r + s : 2 * r + s + 1, :] = combine[8 * s + r : 8 * s + r + 1]
    combine = ordered[...]
    state[...] = jnp.zeros_like(state)
    combine_high = combine.astype(BF)
    combine_low = (combine - combine_high.astype(F32)).astype(BF)
    mine = pl.ds(pl.multiple_of(t * PART, 128), PART)
    res[...] = jnp.zeros_like(res)
    for r in range(ROWS):
        both = res_raw[r].astype(F32)
        res[r : r + 1, :] = both[0:1]
        res[8 + r : 9 + r, :] = both[1:2]
    res_sum = jnp.sum(res[...], axis=1, keepdims=True)
    res_mine = res[:, mine]
    gain_mine = gain_ref[:, mine]

    def slots(row, slot):
        rank = lax.rem(slot, 16)
        return jnp.where((row == CAP * lax.div(slot, 16) + rank) & (rank < CAP), 1.0, 0.0).astype(BF)

    spans = (16 * NEAR, 16 * (EXPERTS - NEAR))
    packing = [slots(iota((n, w), 0), iota((n, w), 1)) for (_, n), w in zip(GROUPS, spans)]
    unpacking = [slots(iota((w, n), 1), iota((w, n), 0)) for (_, n), w in zip(GROUPS, spans)]
    acc[...] = jnp.zeros_like(acc)
    vacc[...] = jnp.zeros_like(vacc)
    att[...] = jnp.zeros_like(att)
    weights_in[0].wait()

    settle(a_recv.at[pl.ds(0, 15)], one_rs.at[0])

    stats = a_recv[:, 48:64, :].astype(F32)
    tops, totals = stats[:, 0:8], stats[:, 8:16]
    top = jnp.max(tops, axis=0, keepdims=True)
    scale = jnp.exp(tops - top)
    whole = jnp.sum(scale * totals, axis=0, keepdims=True)
    scale = scale / jnp.maximum(whole, 1e-30)
    fcol[...] = jnp.transpose(scale.reshape(128, 128))
    columns = fcol[pl.ds(pl.multiple_of(8 * t, 8), 8), :]
    for pair in range(3):
        both = a_recv[:, 16 * pair : 16 * pair + 16, :].astype(F32)
        for half in range(2):
            r = 2 * pair + half
            joined = jnp.zeros((8, 128), F32)
            for s in range(16):
                joined += both[s, 8 * half : 8 * half + 8] * columns[:, 8 * s + r : 8 * s + r + 1]
            for h in range(3):
                for s in range(STEPS):
                    att[8 * s + r : 8 * s + r + 1, 128 * h : 128 * h + 128] = joined[
                        2 * h + s : 2 * h + s + 1
                    ]

    attended = att[...].astype(BF)
    proj_sum = jnp.zeros((16, 128), F32)
    for s in range(16):
        part = dot(attended, wout[:, PART * s : PART * s + PART])
        proj[s] = part
        proj_sum = proj_sum + part[:, 0:128] + part[:, 128:256] + part[:, 256:384]
    proj_sum = jnp.sum(proj_sum, axis=1, keepdims=True)
    diagonal = jnp.sum(jnp.where(token_row == slot_lane, proj_sum, 0.0), axis=0, keepdims=True)
    high = diagonal.astype(BF).astype(F32)
    low = diagonal - high
    head = jnp.where(token_row == 6, high, jnp.where(token_row == 7, low, 0.0))
    head = jnp.concatenate([head, jnp.zeros((16, PART - 128), F32)], axis=1)

    def b_copy(i):
        to = plane_peer(i)
        return remote(b_send.at[to], b_recv.at[t], sent.at[1], one_rs.at[1], (b, to))

    for i in FAR_PLANE:
        to = plane_peer(i)
        b_send[to] = (proj[to] + head).astype(BF)
        b_copy(i).start()
    b_recv[t] = (proj[t] + head).astype(BF)
    settle(b_recv.at[pl.ds(0, 15)], one_rs.at[1])

    summed = jnp.sum(b_recv[...].astype(F32), axis=0)
    spread = jnp.where(token_row == slot_lane, summed[6:7, 0:128] + summed[7:8, 0:128], 0.0)
    mean = (jnp.sum(spread, axis=1, keepdims=True) + res_sum) * (1.0 / D)
    real = lax.rem(iota((16, PART), 0), 8) < ROWS
    hidden = jnp.where(real, summed + res_mine, 0.0)
    scaled = jnp.where(real, (hidden - mean) * gain_mine, 0.0).astype(BF)

    z_send[...] = dot(dispatch, scaled).astype(BF).reshape(EXPERTS, 16, PART)

    def z_copy(p):
        to = wrap(z + ORDER[p], 8)
        return remote(z_send.at[to], z_recv.at[p], sent.at[2], z_rs.at[int(p >= NEAR)], (2 * to + c, t))

    for p in range(7, 0, -1):
        z_copy(p).start()
    z_recv[0] = z_send[z]

    def rows_of(s, group):
        lo, n = GROUPS[group]
        return xall.at[c, s, pl.ds(lo, n)]

    def x1_copy(j, group):
        part = rows_of(t, group)
        n = 2 * (j - 1) + group
        return remote(part, part, sent.at[3], x1_rs.at[n], (b, place(c, g, wrap(m + j, 4))))

    def x2_copy(j, d, group):
        part = rows_of(place(c, g, wrap(m - j, 4)), group)
        return remote(part, part, sent.at[4], x2_rs.at[j], (b, place(c, wrap(g + d, 4), m)))

    def xp_copy(j, d):
        s = place(c, wrap(g - d, 4), wrap(m - j, 4))
        late = int(j > 0 and d > 0)
        return remote(xall.at[c, s], xall.at[c, s], sent.at[5], xp_rs.at[late], (partner, t))

    def multiply(offsets):
        found = [4 * wrap(y - i, 4) + wrap(x - j, 4) for i, j in offsets]
        cols = [pl.ds(pl.multiple_of(s * PART, 128), PART) for s in found]
        both = [jnp.concatenate([xall[c, s], xall[1 - c, s]], axis=0) for s in found]
        rows = jnp.concatenate(both, axis=1)
        for u in range(2):
            units = jnp.concatenate([win[u, :, col] for col in cols], axis=1)
            acc[u] += dot(rows, units, NT)
        squares = vacc[...]
        for part, col in zip(both, cols):
            plain = part.astype(F32) * (1.0 / gain_ref[:, col])
            plain = plain * plain
            squares += plain[:, 0:128] + plain[:, 128:256] + plain[:, 256:384]
        vacc[...] = squares

    for group in range(2):
        came = pl.ds(NEAR, EXPERTS - NEAR) if group else pl.ds(1, NEAR - 1)
        settle(z_recv.at[came], z_rs.at[group])
        blocks = z_recv[0:NEAR] if group == 0 else z_recv[NEAR:EXPERTS]
        lo, n = GROUPS[group]
        xall[c, t, lo : lo + n] = dot(
            packing[group], blocks.reshape(spans[group], PART)
        ).astype(BF)
        for j in FAR_RING:
            x1_copy(j, group).start()
        for d in FAR_RING:
            x2_copy(0, d, group).start()
    xp_copy(0, 0).start()
    for r in range(ROWS):
        for s in range(STEPS):
            state[2 * r + s : 2 * r + s + 1, :] = hidden[8 * s + r : 8 * s + r + 1]
    weights_in[1].wait()
    weights_in[2].wait()
    for group in range(2):
        for j in (1, 3, 2):
            x1_copy(j, group).wait_recv()
            for d in FAR_RING:
                x2_copy(j, d, group).start()
            if group:
                xp_copy(j, 0).start()
    settle(xall.at[0, pl.ds(0, 3)], x2_rs.at[0])
    for d in FAR_RING:
        xp_copy(0, d).start()
    settle(xall.at[0, pl.ds(0, 7)], xp_rs.at[0])
    multiply([(0, 0), (0, 1), (0, 2), (0, 3), (1, 0), (2, 0), (3, 0)])
    for j in (1, 3, 2):
        settle(xall.at[0, pl.ds(0, 3)], x2_rs.at[j])
        for d in FAR_RING:
            xp_copy(j, d).start()
    settle(xall.at[0, pl.ds(0, 9)], xp_rs.at[1])
    multiply([(i, j) for i in (1, 2, 3) for j in (1, 2, 3)])

    inverse = lax.rsqrt(jnp.sum(vacc[...], axis=1, keepdims=True) * (1.0 / D) + EPS)
    gate, up = acc[0] * inverse, acc[1] * inverse
    hid[...] = (gate / (1.0 + jnp.exp(-gate)) * up).astype(BF)

    def tiles(lo, found):
        cols = [wdn[:, pl.ds(pl.multiple_of(s * PART, 128), PART)] for s in found]
        slab = dot(hid[lo : lo + PACK], jnp.concatenate(cols, axis=1))
        return [slab[:, PART * i : PART * i + PART] for i in range(4)]

    def q_copy(j):
        part = pl.ds(4 * j, 4)
        return remote(q_send.at[part], q_recv.at[part], sent.at[6], q_rs.at[j], (partner, t))

    def g_copy(j, d, group):
        n = 3 * j + d - 1
        lo, rows = GROUPS[group]
        part = pl.ds(lo, rows)
        return remote(
            g_send.at[n, part], g_recv.at[n, part], sent.at[7], g_rs.at[2 * j + group],
            (b, place(c, wrap(g + d, 4), m)),
        )

    def m_copy(j, group):
        lo, rows = GROUPS[group]
        part = pl.ds(lo, rows)
        return remote(
            m_send.at[j, part], m_recv.at[j, part], sent.at[8], m_rs.at[group],
            (b, place(c, g, wrap(m + j, 4))),
        )

    def y_copy(p):
        to = wrap(z - ORDER[p], 8)
        return remote(y_send.at[p], y_recv.at[z], sent.at[9], one_rs.at[2], (2 * to + c, t))

    for j in MEMBERS:
        found = [place(1 - c, wrap(m + d, 4), wrap(g + j, 4)) for d in range(4)]
        for d, tile in enumerate(tiles(PACK, found)):
            q_send[4 * j + d] = tile.astype(BF)
        q_copy(j).start()
        found = [place(c, wrap(g + d, 4), wrap(m + j, 4)) for d in range(4)]
        for d, tile in enumerate(tiles(0, found)):
            own[4 * j + d] = tile

    for group in (1, 0):
        lo, n = GROUPS[group]
        for j in MEMBERS:
            if group:
                q_copy(j).wait_recv()
            for d in FAR_RING:
                k = 4 * j + d
                g_send[3 * j + d - 1, lo : lo + n] = (
                    own[k, lo : lo + n] + q_recv[k, lo : lo + n].astype(F32)
                ).astype(BF)
                g_copy(j, d, group).start()

    finals = [None, None]
    for group in (1, 0):
        lo, n = GROUPS[group]
        for j in MEMBERS:
            whole = own[4 * j, lo : lo + n] + q_recv[4 * j, lo : lo + n].astype(F32)
            settle(g_recv.at[pl.ds(0, 3), pl.ds(lo, n)], g_rs.at[2 * j + group])
            for d in FAR_RING:
                whole = whole + g_recv[3 * j + d - 1, lo : lo + n].astype(F32)
            if j:
                m_send[j, lo : lo + n] = whole.astype(BF)
                m_copy(j, group).start()
            else:
                finals[group] = whole

    for group in (1, 0):
        lo, n = GROUPS[group]
        final = finals[group]
        settle(m_recv.at[pl.ds(0, 3), pl.ds(lo, n)], m_rs.at[group])
        for j in (1, 3, 2):
            final = final + m_recv[j, lo : lo + n].astype(F32)
        back = dot(unpacking[group], final.astype(BF)).astype(BF)
        if group:
            y_send[NEAR:EXPERTS] = back.reshape(EXPERTS - NEAR, 16, PART)
            for p in range(7, NEAR - 1, -1):
                y_copy(p).start()
        else:
            y_send[0:NEAR] = back.reshape(NEAR, 16, PART)
            for p in range(NEAR - 1, 0, -1):
                y_copy(p).start()
            y_recv[z] = y_send[0]

    settle(a_send.at[pl.ds(0, 15)], sent.at[0])
    settle(b_send.at[pl.ds(0, 15)], sent.at[1])
    settle(z_send.at[pl.ds(0, 7)], sent.at[2])
    settle(xall.at[0, pl.ds(0, 3)], sent.at[3])
    settle(xall.at[0, pl.ds(0, 12)], sent.at[4])
    settle(xall.at[0], sent.at[5])
    settle(q_send, sent.at[6])
    settle(g_send, sent.at[7])
    settle(m_send.at[pl.ds(0, 3)], sent.at[8])

    settle(y_recv.at[pl.ds(0, 7)], one_rs.at[2])
    returned = y_recv[...].reshape(128, PART)
    mix = dot(combine_high, returned) + dot(combine_low, returned)
    out_ref[...] = (state[...] + mix).astype(BF)
    settle(y_send.at[pl.ds(0, 7)], sent.at[9])


def body(queries, new_kv, cache, residual, w_out, norm_gain, routes, route_weight, w_in, w_down):
    fresh = new_kv.reshape(2, ROWS, STEPS, KV, HD).transpose(0, 1, 3, 2, 4)
    fresh = fresh.reshape(2, ROWS, 16, HD)
    w_in_t = w_in.transpose(0, 2, 3, 1).reshape(2, UNITS, D)
    w_down = w_down.reshape(UNITS, D)
    gain = norm_gain.reshape(1, D)
    chosen = routes.transpose(1, 2, 0)
    factors = route_weight.transpose(1, 2, 0)
    hbm = pl.BlockSpec(memory_space=pltpu.HBM)
    dma = pltpu.SemaphoreType.DMA
    vmem = pltpu.VMEM
    out = pl.pallas_call(
        kernel,
        out_shape=jax.ShapeDtypeStruct((16, PART), BF),
        in_specs=[hbm] * 10,
        out_specs=pl.BlockSpec(memory_space=pltpu.VMEM),
        scratch_shapes=[
            vmem((ROWS, STEPS, D), BF),
            vmem((2, ROWS, 128, HD), BF),
            vmem((ROWS, STEPS, D), BF),
            vmem((1, D), F32),
            vmem((STEPS, TOP, ROWS), jnp.int32),
            vmem((STEPS, TOP, ROWS), F32),
            vmem((ROWS, 128, HD), BF),
            vmem((16, D), F32),
            vmem((128, 128), F32),
            vmem((16, 128), F32),
            vmem((2, ROWS, KV, KEYS, HD), BF),
            vmem((PART, D), BF),
            vmem((2, UNITS, D), BF),
            vmem((UNITS, D), BF),
            vmem((16, 64, 128), BF),
            vmem((16, 64, 128), BF),
            vmem((128, 128), F32),
            vmem((128, 128), F32),
            vmem((16, PART), F32),
            vmem((16, 16, PART), F32),
            vmem((16, 16, PART), BF),
            vmem((16, 16, PART), BF),
            vmem((16, PART), F32),
            vmem((EXPERTS, 16, PART), BF),
            vmem((EXPERTS, 16, PART), BF),
            vmem((2, 16, PACK, PART), BF),
            vmem((2, 2 * PACK, UNITS), F32),
            vmem((2 * PACK, 128), F32),
            vmem((2 * PACK, UNITS), BF),
            vmem((16, PACK, PART), F32),
            vmem((16, PACK, PART), BF),
            vmem((16, PACK, PART), BF),
            vmem((12, PACK, PART), BF),
            vmem((12, PACK, PART), BF),
            vmem((4, PACK, PART), BF),
            vmem((4, PACK, PART), BF),
            vmem((EXPERTS, 16, PART), BF),
            vmem((EXPERTS, 16, PART), BF),
            dma((6,)), dma((2, ROWS)), dma((3,)), dma((10,)), dma((3,)),
            dma((2,)), dma((6,)), dma((4,)), dma((2,)), dma((4,)), dma((8,)), dma((2,)),
        ],
        compiler_params=pltpu.CompilerParams(
            collective_id=0, has_side_effects=True, vmem_limit_bytes=56 * 1024 * 1024
        ),
        name="layer",
    )(queries, fresh, cache, residual, w_out, gain, chosen, factors, w_in_t, w_down)
    return out[:12].reshape(ROWS, STEPS, PART)


def solution(mesh):
    return jax.shard_map(
        body,
        mesh=mesh,
        in_specs=(
            P("expert", None, None),
            P(None, "expert", None, None),
            P(None, "expert", None, "tensor", None),
            P("expert", None, None),
            P("tensor", None),
            P(),
            P("expert", None, None),
            P("expert", None, None),
            P("expert", None, None, "tensor"),
            P("expert", "tensor", None),
        ),
        out_specs=P("expert", None, "tensor"),
        check_vma=False,
    )
```
